32 devices in a mesh: ctx: 4 (over y, core), head: 8 (over z, x).
Axes of the slice: x: 2, y: 2, z: 4, core: 2. Of those that a mesh axis runs over, the one named last changes fastest.
Arguments:
- queries: bfloat16 [3072, 2048], P('ctx', 'head'), may hold values from -1.796875 to 1.796875
- keys: bfloat16 [3072, 2048], P('ctx', 'head'), may hold values from -1.796875 to 1.796875
- values: bfloat16 [3072, 2048], P('ctx', 'head'), may hold values from -18 to 18
- cotangent: bfloat16 [3072, 2048], P('ctx', 'head'), may hold values from -6 to 6
- decay_code: int32 [16], P('head'), may hold values from 4 to 32768, as said below
- boundaries: int32 [3072], P('ctx'), may hold values 0 or 1
Outputs:
- output: bfloat16 [3072, 2048], P('ctx', 'head')
- grad_queries: bfloat16 [3072, 2048], P('ctx', 'head')
- grad_keys: bfloat16 [3072, 2048], P('ctx', 'head')
- grad_values: bfloat16 [3072, 2048], P('ctx', 'head')
The draws below stay inside these ranges and needn't reach their ends.
Inputs may be any that keep to these rules, and one draw needn't show every extreme that they name: Head h's decay per token is 1 - decay_code[h] * 2^-20.
All inputs are finite; a program needn't handle non-finite values. No bound on the sum of `boundaries` on one device may be relied on, other than what follows from the above.
Results may differ from the reference program's by a relative error of at most 0.0061.
Values sent between devices are 32-bit elements; how exact they have to be, the bound alone decides.
No kernel may reach another device: no remote copies, remote signals or barrier semaphores. Data moves between devices by JAX's collectives and lax.ppermute only.
A program may use at most 64 MiB of HBM per device.

```python
import math
import jax
import jax.numpy as jnp
from jax import lax

HEAD = 128
HEADS = 16
BLK = 256
TOKENS = 3072


def draw_values(key, part):
    head_key, entry_key = jax.random.split(key)
    scales = jnp.exp(jax.random.uniform(head_key, (HEADS,), jnp.float32, math.log(0.3), math.log(3.0)))
    base = jax.random.truncated_normal(entry_key, -6.0, 6.0, (TOKENS, HEADS, HEAD), jnp.float32)
    return (base * scales[None, :, None]).reshape(TOKENS, HEADS * HEAD).astype(jnp.bfloat16)


def draw_decay_code(key, part):
    shift_key, base_key, order_key = jax.random.split(key, 3)
    shifts = jnp.clip(jax.random.randint(shift_key, (HEADS,), -8, 13), 0, 12)
    bases = jax.random.randint(base_key, (HEADS,), 4, 9)
    codes = jnp.left_shift(bases, shifts)
    order = jax.random.permutation(order_key, HEADS)
    codes = jnp.where(order == 0, 4, jnp.where(order == 1, 32768, codes))
    return codes.astype(jnp.int32)


def plant(values, key, smallest, top_value):
    extent = values.shape
    spot = [jax.random.randint(jax.random.fold_in(key, axis), (), 0, extent[axis]) for axis in range(len(extent))]
    values = values.at[tuple(spot)].set(smallest)
    longest = extent.index(max(extent))
    spot[longest] = (spot[longest] + 1) % extent[longest]
    return values.at[tuple(spot)].set(top_value)


def level_of(own_key, shape, cuts, low, largest):
    loudness, own = 1.0, jax.random.fold_in(own_key, 6)
    for position, parts in cuts:
        draws = jnp.exp(jax.random.uniform(jax.random.fold_in(own, position), (parts,), jnp.float32, low / len(cuts), largest / len(cuts)))
        loudness = loudness * jnp.repeat(draws, shape[position] // parts).reshape([-1 if axis == position else 1 for axis in range(len(shape))])
    return loudness


def bell_draw(rng, dims, width, bound, cuts=(), kind=jnp.bfloat16):
    gain = level_of(rng, dims, cuts, -0.22, 0.18) if cuts else 1.0
    entries = jax.random.normal(rng, dims, jnp.float32) * width * gain
    return jnp.minimum(jnp.maximum(entries, -bound), bound).astype(kind)


def setup_inputs(seed: int = 0) -> dict:
    arg_keys = jax.random.split(jax.random.key(seed), 7)
    return {
        "queries": bell_draw(arg_keys[0], (TOKENS, HEADS * HEAD), 0.3, 1.796875, ((0, 4), (1, 8))),
        "keys": bell_draw(arg_keys[1], (TOKENS, HEADS * HEAD), 0.3, 1.796875, ((0, 4), (1, 8))),
        "values": draw_values(jax.random.fold_in(arg_keys[6], 71), 0),
        "cotangent": bell_draw(arg_keys[3], (TOKENS, HEADS * HEAD), 1.0, 6.0, ((0, 4), (1, 8))),
        "decay_code": draw_decay_code(jax.random.fold_in(arg_keys[6], 71), 0),
        "boundaries": plant((jax.random.randint(arg_keys[5], (TOKENS,), 0, 1024) < 1).astype(jnp.int32), jax.random.fold_in(arg_keys[5], 1), 0, 1),
    }


LOG_HALF = math.log(0.5)
EPSILON = 1e-06

def rounded(array):
    return lax.optimization_barrier(array.astype(jnp.bfloat16)).astype(jnp.float32)

def block_decays(decay_code, boundaries, block_count):
    rates = jnp.log1p(decay_code.astype(jnp.float32) * -2.0 ** (-20))
    log_steps = rates[None, :] + boundaries.astype(jnp.float32)[:, None] * LOG_HALF
    return jnp.cumsum(log_steps.reshape(block_count, BLK, rates.shape[0]), axis=1)

def decay_grid(levels):
    causal = jnp.arange(BLK)[:, None] >= jnp.arange(BLK)[None, :]
    spread = levels.T[:, :, None] - levels.T[:, None, :]
    return (causal, jnp.exp(jnp.where(causal[None], spread, 0.0)))

def reference(queries, keys, values, cotangent, decay_code, boundaries):
    token_count, full_width = queries.shape
    head_count = decay_code.shape[0]
    head_size = full_width // head_count
    block_count = token_count // BLK
    cumulative = block_decays(decay_code, boundaries, block_count)
    shape_four = (block_count, BLK, head_count, head_size)
    query_blocks = queries.reshape(shape_four)
    key_blocks = keys.reshape(shape_four)
    value_blocks = values.reshape(shape_four)
    zero_state = jnp.zeros((head_count, head_size, head_size), jnp.float32)

    def forward_step(state, block):
        query_block, key_block, value_block, levels = block
        query_float = query_block.astype(jnp.float32)
        key_float = key_block.astype(jnp.float32)
        value_float = value_block.astype(jnp.float32)
        totals = levels[-1]
        causal, decays = decay_grid(levels)
        scores = jnp.einsum('ihe,jhe->hij', query_float, key_float)
        weights = rounded(jnp.where(causal[None], scores * decays, 0.0))
        held_state = rounded(state)
        attended = jnp.einsum('hij,jhe->ihe', weights, value_float) + jnp.exp(levels)[:, :, None] * jnp.einsum('ihd,hde->ihe', query_float, held_state)
        scaled_keys = rounded(key_float * jnp.exp(totals[None, :] - levels)[:, :, None])
        state = jnp.exp(totals)[:, None, None] * state + jnp.einsum('jhd,jhe->hde', scaled_keys, value_float)
        return (state, (attended, held_state.astype(jnp.bfloat16)))
    unused, (attended, held_states) = lax.scan(forward_step, zero_state, (query_blocks, key_blocks, value_blocks, cumulative))
    attended = attended.reshape(token_count, full_width)
    scale = lax.rsqrt(lax.optimization_barrier(jnp.sum(attended * attended, axis=1)) / full_width + EPSILON)
    normed = attended * scale[:, None]
    output = normed.astype(jnp.bfloat16)
    grad_float = cotangent.astype(jnp.float32)
    slope = lax.optimization_barrier(jnp.sum(grad_float * normed, axis=1))
    grad_attended = rounded(scale[:, None] * (grad_float - normed * (slope / full_width)[:, None]))
    grad_blocks = grad_attended.reshape(shape_four)

    def backward_step(grad_state, block):
        query_block, key_block, value_block, grad_block, levels, held_state = block
        query_float = query_block.astype(jnp.float32)
        key_float = key_block.astype(jnp.float32)
        value_float = value_block.astype(jnp.float32)
        held_float = held_state.astype(jnp.float32)
        totals = levels[-1]
        causal, decays = decay_grid(levels)
        scores = jnp.einsum('ihe,jhe->hij', query_float, key_float)
        weights = rounded(jnp.where(causal[None], scores * decays, 0.0))
        grad_scores = jnp.einsum('ihe,jhe->hij', grad_block, value_float)
        grad_weights = rounded(jnp.where(causal[None], grad_scores * decays, 0.0))
        held_grad = rounded(grad_state)
        beyond = jnp.exp(totals[None, :] - levels)[:, :, None]
        grad_q = jnp.einsum('hij,jhd->ihd', grad_weights, key_float) + jnp.exp(levels)[:, :, None] * jnp.einsum('ihe,hde->ihd', grad_block, held_float)
        grad_k = jnp.einsum('hij,ihd->jhd', grad_weights, query_float) + beyond * jnp.einsum('jhe,hde->jhd', value_float, held_grad)
        grad_v = jnp.einsum('hij,ihe->jhe', weights, grad_block) + beyond * jnp.einsum('jhd,hde->jhe', key_float, held_grad)
        lifted = rounded(query_float * jnp.exp(levels)[:, :, None])
        grad_state = jnp.exp(totals)[:, None, None] * grad_state + jnp.einsum('ihd,ihe->hde', lifted, grad_block)
        return (grad_state, (grad_q, grad_k, grad_v))
    unused, (grad_q, grad_k, grad_v) = lax.scan(backward_step, zero_state, (query_blocks, key_blocks, value_blocks, grad_blocks, cumulative, held_states), reverse=True)
    return (output, grad_q.reshape(token_count, full_width).astype(jnp.bfloat16), grad_k.reshape(token_count, full_width).astype(jnp.bfloat16), grad_v.reshape(token_count, full_width).astype(jnp.bfloat16))
```

```python
import functools
import math

import jax
import jax.numpy as jnp
from jax import lax
from jax.experimental import pallas as pl
from jax.experimental.pallas import tpu as pltpu
from jax.sharding import PartitionSpec as P

BLK = 256
LANES = 128
LOG_TWO = math.log(2.0)
EPSILON = 1e-06
F32 = jnp.float32
BF16 = jnp.bfloat16

NN = (((1,), (0,)), ((), ()))
NT = (((1,), (1,)), ((), ()))
TN = (((0,), (0,)), ((), ()))


def mm(a, b, dims=NN):
    return lax.dot_general(a, b, dims, preferred_element_type=F32)


def iota(shape, axis):
    return lax.broadcasted_iota(jnp.int32, shape, axis)


def up8(n):
    return -(-n // 8) * 8


def halves(x):
    head = x.astype(BF16)
    return head, (x - head.astype(F32)).astype(BF16)


class Steps:
    def __init__(self, bnd_ref, code_ref, blocks, heads):
        self.blocks, self.heads, self.size = blocks, heads, blocks * heads
        rows = up8(self.size)
        per = BLK // LANES
        bnd = bnd_ref[...].astype(F32)
        parts = []
        for b in range(blocks):
            row = jnp.concatenate([bnd[b * per + i : b * per + i + 1] for i in range(per)], axis=1)
            parts += [row] * heads
        if rows > self.size:
            parts.append(jnp.zeros((rows - self.size, BLK), F32))
        marks = jnp.concatenate(parts, axis=0).astype(BF16)
        upper = (iota((BLK, BLK), 0) <= iota((BLK, BLK), 1)).astype(F32).astype(BF16)
        self.count = mm(marks, upper)
        count_all = mm(marks, jnp.ones((BLK, BLK), BF16))
        which = iota((rows, BLK), 0)
        code = jnp.zeros((rows, BLK), F32)
        for h in range(heads):
            code = jnp.where(which % heads == h, code_ref[h].astype(F32), code)
        self.rate = jnp.log1p(code * -(2.0 ** (-20)))
        place = (iota((rows, BLK), 1) + 1).astype(F32)
        self.level = self.rate * place - LOG_TWO * self.count
        self.total = self.rate * float(BLK) - LOG_TWO * count_all
        self.growth = jnp.exp(self.level)
        self.beyond = jnp.exp(self.total - self.level)
        self.decay = jnp.exp(self.total)

    def row(self, a, b, h):
        r = b * self.heads + h
        return a[r : r + 1]

    def device_total(self, h):
        return sum(self.row(self.total, b, h) for b in range(self.blocks))[:, :LANES]

    def columns(self, a, head_size):
        head, rest = halves(a)
        both = jnp.concatenate([head.astype(F32), rest.astype(F32)], axis=0).astype(BF16)
        rows, width = a.shape[0], self.heads * head_size
        result = []
        for b in range(self.blocks):
            wanted = b * self.heads + iota((2 * rows, width), 1) // head_size
            pick = (iota((2 * rows, width), 0) % rows == wanted).astype(F32).astype(BF16)
            result.append(mm(both, pick, TN))
        return result

    def decays(self, b):
        rows = self.count.shape[0]
        pick = (iota((rows, BLK), 0) == b * self.heads).astype(F32).astype(BF16)
        count_i = mm(self.count.astype(BF16), pick, TN)
        halved = LOG_TWO * (count_i - self.row(self.count, b, 0))
        apart = iota((BLK, BLK), 0) - iota((BLK, BLK), 1)
        causal = apart >= 0
        steps = apart.astype(F32)
        return causal, [
            jnp.exp(jnp.where(causal, self.row(self.rate, b, h) * steps - halved, 0.0))
            for h in range(self.heads)
        ]


def incoming(payloads, place, masks, h, head_size, heads, reverse):
    at = heads * head_size + h
    totals = [p[at : at + 1, :] for p in payloads]
    sources = [place ^ m for m in masks]

    def before(a, b):
        return a > b if reverse else a < b

    result = jnp.zeros((head_size, head_size), F32)
    for i, m in enumerate(masks):
        if m == 0:
            continue
        inner = jnp.zeros_like(totals[0])
        for j, other in enumerate(masks):
            if other in (0, m):
                continue
            between = jnp.logical_and(before(sources[i], sources[j]), before(sources[j], place))
            inner = inner + jnp.where(between, totals[j], 0.0)
        weight = jnp.where(before(sources[i], place), jnp.exp(inner), 0.0)
        result = result + weight * payloads[i][h * head_size : (h + 1) * head_size, :]
    return result


def store_totals(payload_ref, st, head_size):
    rest = [st.device_total(h) for h in range(st.heads)]
    pad = up8(st.heads) - st.heads
    if pad:
        rest.append(jnp.zeros((pad, LANES), F32))
    payload_ref[st.heads * head_size :, :] = jnp.concatenate(rest, axis=0)


def sizes(x_ref, code_ref):
    tokens, width = x_ref.shape
    heads = code_ref.shape[0]
    return tokens // BLK, heads, width // heads


def block(ref, b, h, e):
    return ref[b * BLK : (b + 1) * BLK, h * e : (h + 1) * e]


def states_kernel(code_ref, bnd_ref, k_ref, v_ref, payload_ref, local_ref):
    nb, heads, e = sizes(k_ref, code_ref)
    st = Steps(bnd_ref, code_ref, nb, heads)
    for h in range(heads):
        running = None
        for b in range(nb):
            scaled = (block(k_ref, b, h, e).T.astype(F32) * st.row(st.beyond, b, h)).astype(BF16)
            term = mm(scaled, block(v_ref, b, h, e))
            running = term if running is None else st.row(st.decay, b, h)[:, :e] * running + term
            if b < nb - 1:
                local_ref[b, h] = running
        payload_ref[h * e : (h + 1) * e, :] = running
    store_totals(payload_ref, st, e)


def within_kernel(code_ref, bnd_ref, q_ref, k_ref, v_ref, w_ref, within_ref):
    nb, heads, e = sizes(k_ref, code_ref)
    st = Steps(bnd_ref, code_ref, nb, heads)
    for b in range(nb):
        causal, decays = st.decays(b)
        for h in range(heads):
            scores = mm(block(q_ref, b, h, e), block(k_ref, b, h, e), NT)
            weights = jnp.where(causal, scores * decays[h], 0.0).astype(BF16)
            w_ref[b, h] = weights
            within_ref[b * BLK : (b + 1) * BLK, h * e : (h + 1) * e] = mm(
                weights, block(v_ref, b, h, e)
            )


def attend_kernel(masks, code_ref, place_ref, bnd_ref, q_ref, cot_ref, within_ref, local_ref, *refs):
    payloads, (held_ref, att_ref, sums_ref) = refs[: len(masks)], refs[len(masks) :]
    nb, heads, e = sizes(q_ref, code_ref)
    st = Steps(bnd_ref, code_ref, nb, heads)
    growth = st.columns(st.growth, e)
    for h in range(heads):
        arrived = incoming(payloads, place_ref[0], masks, h, e, heads, False)
        ahead = jnp.zeros((1, BLK), F32)
        for b in range(nb):
            state = jnp.exp(ahead)[:, :e] * arrived
            if b:
                state = state + local_ref[b - 1, h]
            ahead = ahead + st.row(st.total, b, h)
            held_ref[b, h] = state.astype(BF16)
    ones = jnp.ones((8, heads * e), BF16)
    squares, crosses = [], []
    for b in range(nb):
        rows = slice(b * BLK, (b + 1) * BLK)
        carried = jnp.concatenate(
            [mm(block(q_ref, b, h, e), held_ref[b, h]) for h in range(heads)], axis=1
        )
        att = within_ref[rows, :] + growth[b] * carried
        att_ref[rows, :] = att
        for dest, term in ((squares, att * att), (crosses, att * cot_ref[rows, :].astype(F32))):
            dest.append(sum(mm(ones, part, NT) for part in halves(term))[:1])
    parts = squares + crosses
    if up8(2 * nb) > 2 * nb:
        parts.append(jnp.zeros((up8(2 * nb) - 2 * nb, BLK), F32))
    sums_ref[...] = jnp.concatenate(parts, axis=0)


def norm_factors(sums, st, full_width):
    nb = st.blocks
    squares, crosses = sums[:nb], sums[nb : 2 * nb]
    scale = lax.rsqrt(squares / full_width + EPSILON)
    lean = scale * scale * crosses / full_width
    return scale, lean


def spread(rows_of, width):
    count = rows_of[0].shape[0]
    stacked = jnp.concatenate(rows_of, axis=0)
    have = stacked.shape[0]
    if up8(have) > have:
        stacked = jnp.concatenate([stacked, jnp.zeros((up8(have) - have, BLK), F32)], axis=0)
    rows = stacked.shape[0]
    head, rest = halves(stacked)
    both = jnp.concatenate([head.astype(F32), rest.astype(F32)], axis=0).astype(BF16)
    result = []
    for r in range(have):
        pick = (iota((2 * rows, width), 0) % rows == r).astype(F32).astype(BF16)
        result.append(mm(both, pick, TN))
    return [result[i * count : (i + 1) * count] for i in range(len(rows_of))]


def grad_kernel(full_width, parts, code_ref, bnd_ref, q_ref, cot_ref, att_ref, *refs):
    sums_refs, (g_ref, total_ref, payload_ref, local_ref) = refs[:parts], refs[parts:]
    nb, heads, e = sizes(q_ref, code_ref)
    st = Steps(bnd_ref, code_ref, nb, heads)
    sums = sum(ref[...] for ref in sums_refs)
    total_ref[...] = sums
    scale, lean = spread(norm_factors(sums, st, full_width), heads * e)
    for b in range(nb):
        rows = slice(b * BLK, (b + 1) * BLK)
        g_ref[rows, :] = (
            scale[b] * (cot_ref[rows, :].astype(F32) - att_ref[rows, :] * lean[b])
        ).astype(BF16)
    for h in range(heads):
        running = None
        for b in reversed(range(nb)):
            lifted = (block(q_ref, b, h, e).T.astype(F32) * st.row(st.growth, b, h)).astype(BF16)
            term = mm(lifted, block(g_ref, b, h, e))
            running = term if running is None else st.row(st.decay, b, h)[:, :e] * running + term
            if b:
                local_ref[b - 1, h] = running
        payload_ref[h * e : (h + 1) * e, :] = running
    store_totals(payload_ref, st, e)


def inner_grads_kernel(
    full_width, code_ref, bnd_ref, q_ref, k_ref, v_ref, g_ref, w_ref, held_ref, att_ref, total_ref,
    out_ref, gq_ref, gk_ref, gv_ref,
):
    nb, heads, e = sizes(q_ref, code_ref)
    st = Steps(bnd_ref, code_ref, nb, heads)
    scale = lax.rsqrt(total_ref[:nb, :] / full_width + EPSILON)
    (scale,) = spread((scale,), heads * e)
    growth = st.columns(st.growth, e)
    for b in range(nb):
        rows = slice(b * BLK, (b + 1) * BLK)
        out_ref[rows, :] = (att_ref[rows, :] * scale[b]).astype(BF16)
        causal, decays = st.decays(b)
        for h in range(heads):
            cols = slice(h * e, (h + 1) * e)
            g = block(g_ref, b, h, e)
            scores = mm(g, block(v_ref, b, h, e), NT)
            gw = jnp.where(causal, scores * decays[h], 0.0).astype(BF16)
            gq = mm(gw, block(k_ref, b, h, e)) + growth[b][:, cols] * mm(g, held_ref[b, h], NT)
            gq_ref[rows, cols] = gq.astype(BF16)
            gk_ref[rows, cols] = mm(gw, block(q_ref, b, h, e), TN)
            gv_ref[rows, cols] = mm(w_ref[b, h], g, TN)


def outer_grads_kernel(
    masks, code_ref, place_ref, bnd_ref, k_ref, v_ref, gk_part_ref, gv_part_ref, local_ref, *refs
):
    payloads, (gk_ref, gv_ref) = refs[: len(masks)], refs[len(masks) :]
    nb, heads, e = sizes(k_ref, code_ref)
    st = Steps(bnd_ref, code_ref, nb, heads)
    beyond = st.columns(st.beyond, e)
    for h in range(heads):
        cols = slice(h * e, (h + 1) * e)
        arrived = incoming(payloads, place_ref[0], masks, h, e, heads, True)
        behind = jnp.zeros((1, BLK), F32)
        for b in reversed(range(nb)):
            rows = slice(b * BLK, (b + 1) * BLK)
            state = jnp.exp(behind)[:, :e] * arrived
            if b < nb - 1:
                state = state + local_ref[b, h]
            behind = behind + st.row(st.total, b, h)
            held = state.astype(BF16)
            far = beyond[b][:, cols]
            gk = gk_part_ref[rows, cols] + far * mm(block(v_ref, b, h, e), held, NT)
            gk_ref[rows, cols] = gk.astype(BF16)
            gv = gv_part_ref[rows, cols] + far * mm(block(k_ref, b, h, e), held)
            gv_ref[rows, cols] = gv.astype(BF16)


def call(kernel, name, args, outs, flops):
    smem = [a.ndim == 1 for a in args]
    traffic = sum(a.size * a.dtype.itemsize for a in args) + sum(
        math.prod(s) * jnp.dtype(d).itemsize for s, d in outs
    )
    return pl.pallas_call(
        kernel,
        out_shape=[jax.ShapeDtypeStruct(s, d) for s, d in outs],
        in_specs=[
            pl.BlockSpec(memory_space=pltpu.SMEM if s else pltpu.VMEM) for s in smem
        ],
        out_specs=[pl.BlockSpec(memory_space=pltpu.VMEM) for _ in outs],
        compiler_params=pltpu.CompilerParams(vmem_limit_bytes=40 * 2**20),
        cost_estimate=pl.CostEstimate(flops=flops, bytes_accessed=traffic, transcendentals=0),
        name=name,
    )(*args)


def swap(a, axis, mask):
    return lax.ppermute(a, axis, [(i, i ^ mask) for i in range(lax.axis_size(axis))])


def gather_states(payload):
    masks, held = [0], [payload]
    bit = lax.axis_size("ctx") // 2
    while bit:
        held += [swap(a, "ctx", bit) for a in held]
        masks += [m | bit for m in masks]
        bit //= 2
    return masks, held


def sum_over_heads(sums):
    size = lax.axis_size("head")
    parts, bit, width = [sums], 1, 2
    while bit < size:
        own = functools.reduce(jnp.add, parts)
        width = min(width, size // bit)
        parts = [own] + [swap(own, "head", bit * i) for i in range(1, width)]
        bit, width = bit * width, 4
    return parts


def shards(queries, keys, values, cotangent, decay_code, boundaries):
    tokens, width = queries.shape
    heads = decay_code.shape[0]
    e = width // heads
    nb = tokens // BLK
    full_width = width * lax.axis_size("head")
    bnd = boundaries.reshape(tokens // LANES, LANES)
    place = lax.axis_index("ctx").astype(jnp.int32).reshape(1)
    payload = ((heads * e + up8(heads), LANES), F32)
    local = ((max(nb - 1, 1), heads, e, e), F32)
    big = 2 * tokens * heads * e * BLK
    small = 2 * tokens * heads * e * e

    state, prefix = call(
        states_kernel, "states", (decay_code, bnd, keys, values), (payload, local), small
    )
    masks, states = gather_states(state)
    weights, within = call(
        within_kernel, "within", (decay_code, bnd, queries, keys, values),
        (((nb, heads, BLK, BLK), BF16), ((tokens, width), F32)), 2 * big,
    )
    held, attended, sums = call(
        functools.partial(attend_kernel, masks), "attend",
        (decay_code, place, bnd, queries, cotangent, within, prefix, *states),
        (((nb, heads, e, e), BF16), ((tokens, width), F32), ((up8(2 * nb), BLK), F32)), small,
    )
    sums = sum_over_heads(sums)
    grad, totals, grad_state, suffix = call(
        functools.partial(grad_kernel, full_width, len(sums)), "grad",
        (decay_code, bnd, queries, cotangent, attended, *sums),
        (((tokens, width), BF16), ((up8(2 * nb), BLK), F32), payload, local), small,
    )
    masks, grad_states = gather_states(grad_state)
    output, grad_queries, gk_part, gv_part = call(
        functools.partial(inner_grads_kernel, full_width), "inner_grads",
        (decay_code, bnd, queries, keys, values, grad, weights, held, attended, totals),
        (((tokens, width), BF16), ((tokens, width), BF16), ((tokens, width), F32), ((tokens, width), F32)),
        4 * big + small,
    )
    grad_keys, grad_values = call(
        functools.partial(outer_grads_kernel, masks), "outer_grads",
        (decay_code, place, bnd, keys, values, gk_part, gv_part, suffix, *grad_states),
        (((tokens, width), BF16), ((tokens, width), BF16)), 2 * small,
    )
    return output, grad_queries, grad_keys, grad_values


def solution(mesh):
    both = P("ctx", "head")
    return jax.shard_map(
        shards,
        mesh=mesh,
        in_specs=(both, both, both, both, P("head"), P("ctx")),
        out_specs=(both, both, both, both),
        check_vma=False,
    )
```

```python
import functools
import math

import jax
import jax.numpy as jnp
from jax import lax
from jax.experimental import pallas as pl
from jax.experimental.pallas import tpu as pltpu
from jax.sharding import PartitionSpec as P

BLK = 256
LANES = 128
LOG_TWO = math.log(2.0)
EPSILON = 1e-06
F32 = jnp.float32
BF16 = jnp.bfloat16

NN = (((1,), (0,)), ((), ()))
NT = (((1,), (1,)), ((), ()))
TN = (((0,), (0,)), ((), ()))


def mm(a, b, dims=NN):
    return lax.dot_general(a, b, dims, preferred_element_type=F32)


def iota(shape, axis):
    return lax.broadcasted_iota(jnp.int32, shape, axis)


def up8(n):
    return -(-n // 8) * 8


def halves(x):
    head = x.astype(BF16)
    return head, (x - head.astype(F32)).astype(BF16)


ROWS = ("growth", "beyond", "decay", "total", "count", "rate")


def factor_rows(bnd_ref, code_ref, blocks, heads):
    rows = up8(blocks * heads)
    per = BLK // LANES
    bnd = bnd_ref[...].astype(F32)
    parts = []
    for b in range(blocks):
        row = jnp.concatenate([bnd[b * per + i : b * per + i + 1] for i in range(per)], axis=1)
        parts += [row] * heads
    if rows > blocks * heads:
        parts.append(jnp.zeros((rows - blocks * heads, BLK), F32))
    marks = jnp.concatenate(parts, axis=0).astype(BF16)
    upper = (iota((BLK, BLK), 0) <= iota((BLK, BLK), 1)).astype(F32).astype(BF16)
    count = mm(marks, upper)
    count_all = mm(marks, jnp.ones((BLK, BLK), BF16))
    which = iota((rows, BLK), 0)
    code = jnp.zeros((rows, BLK), F32)
    for h in range(heads):
        code = jnp.where(which % heads == h, code_ref[h].astype(F32), code)
    rate = jnp.log1p(code * -(2.0 ** (-20)))
    place = (iota((rows, BLK), 1) + 1).astype(F32)
    level = rate * place - LOG_TWO * count
    total = rate * float(BLK) - LOG_TWO * count_all
    return jnp.exp(level), jnp.exp(total - level), jnp.exp(total), total, count, rate


class Factors:
    def __init__(self, ref, blocks, heads):
        self.ref, self.blocks, self.heads, self.rows = ref, blocks, heads, up8(blocks * heads)

    def all(self, name):
        at = ROWS.index(name) * self.rows
        return self.ref[at : at + self.rows, :]

    def row(self, name, b, h, lanes=BLK):
        at = ROWS.index(name) * self.rows + b * self.heads + h
        return self.ref[at : at + 1, :lanes]

    def device_total(self, h):
        return sum(self.row("total", b, h, LANES) for b in range(self.blocks))

    def decays(self, b):
        pick = (iota((self.rows, BLK), 0) == b * self.heads).astype(F32).astype(BF16)
        count_i = mm(self.all("count").astype(BF16), pick, TN)
        halved = LOG_TWO * (count_i - self.row("count", b, 0))
        apart = iota((BLK, BLK), 0) - iota((BLK, BLK), 1)
        causal = apart >= 0
        steps = apart.astype(F32)
        return causal, [
            jnp.exp(jnp.where(causal, self.row("rate", b, h) * steps - halved, 0.0))
            for h in range(self.heads)
        ]


def spread(a, wanted, width):
    head, rest = halves(a)
    both = jnp.concatenate([head.astype(F32), rest.astype(F32)], axis=0).T.astype(BF16)
    rows = a.shape[0]
    result = []
    for some in wanted:
        lane, row = iota((2 * rows, width), 1), iota((2 * rows, width), 0) % rows
        pick = jnp.zeros((2 * rows, width), F32)
        for i, r in enumerate(some):
            share = lane // (width // len(some)) == i
            pick = jnp.where(jnp.logical_and(share, row == r), 1.0, pick)
        result.append(mm(both, pick.astype(BF16)))
    return result


def incoming(payloads, place, masks, h, head_size, heads, reverse):
    at = heads * head_size + h
    totals = [p[at : at + 1, :] for p in payloads]
    sources = [place ^ m for m in masks]

    def before(a, b):
        return a > b if reverse else a < b

    result = jnp.zeros((head_size, head_size), F32)
    for i, m in enumerate(masks):
        if m == 0:
            continue
        inner = jnp.zeros_like(totals[0])
        for j, other in enumerate(masks):
            if other in (0, m):
                continue
            between = jnp.logical_and(before(sources[i], sources[j]), before(sources[j], place))
            inner = inner + jnp.where(between, totals[j], 0.0)
        weight = jnp.where(before(sources[i], place), jnp.exp(inner), 0.0)
        result = result + weight * payloads[i][h * head_size : (h + 1) * head_size, :]
    return result


def store_totals(payload_ref, fac, head_size):
    rest = [fac.device_total(h) for h in range(fac.heads)]
    pad = up8(fac.heads) - fac.heads
    if pad:
        rest.append(jnp.zeros((pad, LANES), F32))
    payload_ref[fac.heads * head_size :, :] = jnp.concatenate(rest, axis=0)


def block(ref, b, h, e):
    return ref[b * BLK : (b + 1) * BLK, h * e : (h + 1) * e]


def states_kernel(
    dims, code_in, bnd_in, q_in, k_in, v_in, cot_in,
    payload_ref, local_ref, factors_ref, q_ref, k_ref, v_ref, cot_ref, code_ref, bnd_ref, sems,
):
    nb, heads, e = dims
    pairs = (
        (code_in, code_ref), (bnd_in, bnd_ref), (k_in, k_ref), (v_in, v_ref), (q_in, q_ref), (cot_in, cot_ref),
    )
    copies = [pltpu.make_async_copy(s, d, sems.at[i]) for i, (s, d) in enumerate(pairs)]
    for c in copies:
        c.start()
    copies[0].wait()
    copies[1].wait()
    made = factor_rows(bnd_ref, code_ref, nb, heads)
    rows = up8(nb * heads)
    for i, a in enumerate(made):
        factors_ref[i * rows : (i + 1) * rows, :] = a
    fac = Factors(factors_ref, nb, heads)
    store_totals(payload_ref, fac, e)
    copies[2].wait()
    copies[3].wait()
    for h in range(heads):
        running = None
        for b in range(nb):
            scaled = (block(k_ref, b, h, e).T.astype(F32) * fac.row("beyond", b, h)).astype(BF16)
            term = mm(scaled, block(v_ref, b, h, e))
            running = term if running is None else fac.row("decay", b, h, e) * running + term
            if b < nb - 1:
                local_ref[b, h] = running
        payload_ref[h * e : (h + 1) * e, :] = running
    copies[4].wait()
    copies[5].wait()


def within_kernel(dims, factors_ref, q_ref, k_ref, v_ref, w_ref, within_ref, growth_ref, beyond_ref):
    nb, heads, e = dims
    fac = Factors(factors_ref, nb, heads)
    wanted = [[b * heads + h for h in range(heads)] for b in range(nb)]
    for name, ref in (("growth", growth_ref), ("beyond", beyond_ref)):
        for b, a in enumerate(spread(fac.all(name), wanted, heads * e)):
            ref[b * BLK : (b + 1) * BLK, :] = a
    for b in range(nb):
        causal, decays = fac.decays(b)
        for h in range(heads):
            scores = mm(block(q_ref, b, h, e), block(k_ref, b, h, e), NT)
            weights = jnp.where(causal, scores * decays[h], 0.0).astype(BF16)
            w_ref[b, h] = weights
            within_ref[b * BLK : (b + 1) * BLK, h * e : (h + 1) * e] = mm(
                weights, block(v_ref, b, h, e)
            )


def row_sums(a):
    width = a.shape[1]
    narrow = sum(a[:, i : i + LANES] for i in range(0, width, LANES))
    return jnp.sum(narrow.T, axis=0, keepdims=True)


def attend_kernel(
    dims, masks, factors_ref, q_ref, cot_ref, within_ref, growth_ref, local_ref, *refs
):
    payloads, (held_ref, att_ref, sums_ref) = refs[: len(masks)], refs[len(masks) :]
    nb, heads, e = dims
    fac = Factors(factors_ref, nb, heads)
    for h in range(heads):
        arrived = incoming(payloads, lax.axis_index("ctx"), masks, h, e, heads, False)
        ahead = jnp.zeros((1, e), F32)
        for b in range(nb):
            state = jnp.exp(ahead) * arrived
            if b:
                state = state + local_ref[b - 1, h]
            ahead = ahead + fac.row("total", b, h, e)
            held_ref[b, h] = state.astype(BF16)
    squares, crosses = [], []
    for b in range(nb):
        rows = slice(b * BLK, (b + 1) * BLK)
        carried = jnp.concatenate(
            [mm(block(q_ref, b, h, e), held_ref[b, h]) for h in range(heads)], axis=1
        )
        att = within_ref[rows, :] + growth_ref[rows, :] * carried
        att_ref[rows, :] = att
        squares.append(row_sums(att * att))
        crosses.append(row_sums(att * cot_ref[rows, :].astype(F32)))
    parts = squares + crosses
    if up8(2 * nb) > 2 * nb:
        parts.append(jnp.zeros((up8(2 * nb) - 2 * nb, BLK), F32))
    sums_ref[...] = jnp.concatenate(parts, axis=0)


def grad_kernel(dims, full_width, parts, factors_ref, q_ref, cot_ref, att_ref, *refs):
    sums_refs, (g_ref, scale_ref, payload_ref, local_ref) = refs[:parts], refs[parts:]
    nb, heads, e = dims
    fac = Factors(factors_ref, nb, heads)
    sums = sum(ref[...] for ref in sums_refs)
    squares = jnp.where(iota(sums.shape, 0) < nb, sums, 0.0)
    scale = lax.rsqrt(squares / full_width + EPSILON)
    scale_ref[...] = scale
    squared = scale * scale
    lean = jnp.concatenate([squared[:nb], squared[:nb], squared[2 * nb :]], axis=0) * sums / full_width
    factors = jnp.where(iota(sums.shape, 0) < nb, scale, lean)
    columns = spread(factors, [[r] for r in range(2 * nb)], heads * e)
    for b in range(nb):
        rows = slice(b * BLK, (b + 1) * BLK)
        g_ref[rows, :] = (
            columns[b] * (cot_ref[rows, :].astype(F32) - att_ref[rows, :] * columns[nb + b])
        ).astype(BF16)
    for h in range(heads):
        running = None
        for b in reversed(range(nb)):
            lifted = (block(q_ref, b, h, e).T.astype(F32) * fac.row("growth", b, h)).astype(BF16)
            term = mm(lifted, block(g_ref, b, h, e))
            running = term if running is None else fac.row("decay", b, h, e) * running + term
            if b:
                local_ref[b - 1, h] = running
        payload_ref[h * e : (h + 1) * e, :] = running
    store_totals(payload_ref, fac, e)


def inner_grads_kernel(
    dims, factors_ref, q_ref, k_ref, v_ref, g_ref, w_ref, held_ref, att_ref, growth_ref, scale_ref,
    out_hbm, gq_hbm, gk_ref, gv_ref, out_ref, gq_ref, sems,
):
    nb, heads, e = dims
    fac = Factors(factors_ref, nb, heads)
    scale = spread(scale_ref[...], [[b] for b in range(nb)], heads * e)
    copies = []
    for b in range(nb):
        rows = slice(b * BLK, (b + 1) * BLK)
        out_ref[rows, :] = (att_ref[rows, :] * scale[b]).astype(BF16)
        copies.append(
            pltpu.make_async_copy(out_ref.at[rows], out_hbm.at[rows], sems.at[2 * b])
        )
        copies[-1].start()
        causal, decays = fac.decays(b)
        for h in range(heads):
            cols = slice(h * e, (h + 1) * e)
            g = block(g_ref, b, h, e)
            scores = mm(g, block(v_ref, b, h, e), NT)
            gw = jnp.where(causal, scores * decays[h], 0.0).astype(BF16)
            gq = mm(gw, block(k_ref, b, h, e)) + growth_ref[rows, cols] * mm(g, held_ref[b, h], NT)
            gq_ref[rows, cols] = gq.astype(BF16)
            gk_ref[rows, cols] = mm(gw, block(q_ref, b, h, e), TN)
            gv_ref[rows, cols] = mm(w_ref[b, h], g, TN)
        copies.append(
            pltpu.make_async_copy(gq_ref.at[rows], gq_hbm.at[rows], sems.at[2 * b + 1])
        )
        copies[-1].start()
    for c in copies:
        c.wait()


def outer_grads_kernel(
    dims, masks, factors_ref, k_ref, v_ref, gk_part_ref, gv_part_ref, beyond_ref, local_ref, *refs
):
    payloads, (gk_hbm, gv_hbm, gk_ref, gv_ref, sems) = refs[: len(masks)], refs[len(masks) :]
    nb, heads, e = dims
    fac = Factors(factors_ref, nb, heads)
    arrived = [incoming(payloads, lax.axis_index("ctx"), masks, h, e, heads, True) for h in range(heads)]
    behind = [jnp.zeros((1, e), F32) for h in range(heads)]
    copies = []
    for b in reversed(range(nb)):
        rows = slice(b * BLK, (b + 1) * BLK)
        for h in range(heads):
            cols = slice(h * e, (h + 1) * e)
            state = jnp.exp(behind[h]) * arrived[h]
            if b < nb - 1:
                state = state + local_ref[b, h]
            behind[h] = behind[h] + fac.row("total", b, h, e)
            held = state.astype(BF16)
            far = beyond_ref[rows, cols]
            gk = gk_part_ref[rows, cols] + far * mm(block(v_ref, b, h, e), held, NT)
            gk_ref[rows, cols] = gk.astype(BF16)
            gv = gv_part_ref[rows, cols] + far * mm(block(k_ref, b, h, e), held)
            gv_ref[rows, cols] = gv.astype(BF16)
        for i, (s, d) in enumerate(((gk_ref, gk_hbm), (gv_ref, gv_hbm))):
            copies.append(pltpu.make_async_copy(s.at[rows], d.at[rows], sems.at[2 * b + i]))
            copies[-1].start()
    for c in copies:
        c.wait()


def call(kernel, name, args, outs, flops, hbm_in=False, hbm_outs=0, scratch=()):
    traffic = sum(a.size * a.dtype.itemsize for a in args) + sum(
        math.prod(s) * jnp.dtype(d).itemsize for s, d in outs
    )
    hbm = pl.BlockSpec(memory_space=pltpu.HBM)
    vmem, smem = pl.BlockSpec(memory_space=pltpu.VMEM), pl.BlockSpec(memory_space=pltpu.SMEM)
    if hbm_in:
        args = [pltpu.with_memory_space_constraint(a, pltpu.HBM) for a in args]
    return pl.pallas_call(
        kernel,
        out_shape=[(pltpu.HBM if i < hbm_outs else pltpu.VMEM)(s, d) for i, (s, d) in enumerate(outs)],
        in_specs=[hbm if hbm_in else smem if a.ndim == 1 else vmem for a in args],
        out_specs=[hbm if i < hbm_outs else vmem for i in range(len(outs))],
        scratch_shapes=scratch,
        compiler_params=pltpu.CompilerParams(vmem_limit_bytes=16 * 2**20),
        cost_estimate=pl.CostEstimate(flops=flops, bytes_accessed=traffic, transcendentals=0),
        name=name,
    )(*args)


def nothing(*refs):
    pass


def after(a, other):
    anywhere = pl.BlockSpec(memory_space=pltpu.VMEM)
    return pl.pallas_call(
        nothing,
        out_shape=pltpu.VMEM(a.shape, a.dtype),
        in_specs=[anywhere, anywhere],
        out_specs=anywhere,
        input_output_aliases={0: 0},
        compiler_params=pltpu.CompilerParams(vmem_limit_bytes=4 * 2**20),
        name="after",
    )(a, other)


def swap(a, axis, mask):
    return lax.ppermute(a, axis, [(i, i ^ mask) for i in range(lax.axis_size(axis))])


def gather_states(payload, work):
    bit = lax.axis_size("ctx") // 2
    first = swap(payload, "ctx", bit) if bit else payload
    done = work()
    first = after(first, done[-1])
    masks, held = ([0, bit], [payload, first]) if bit else ([0], [payload])
    bit //= 2
    while bit:
        held += [swap(a, "ctx", bit) for a in held]
        masks += [m | bit for m in masks]
        bit //= 2
    return masks, held, done


def sum_over_heads(sums):
    size = lax.axis_size("head")
    parts, bit, width = [sums], 1, 2
    while bit < size:
        own = functools.reduce(jnp.add, parts)
        width = min(width, size // bit)
        parts = [own] + [swap(own, "head", bit * i) for i in range(1, width)]
        bit, width = bit * width, 4
    return parts


def shards(queries, keys, values, cotangent, decay_code, boundaries):
    tokens, width = queries.shape
    heads = decay_code.shape[0]
    e = width // heads
    nb = tokens // BLK
    dims = (nb, heads, e)
    full_width = width * lax.axis_size("head")
    bnd = boundaries.reshape(tokens // LANES, LANES)
    payload = ((heads * e + up8(heads), LANES), F32)
    local = ((max(nb - 1, 1), heads, e, e), F32)
    narrow, wide = ((tokens, width), BF16), ((tokens, width), F32)
    stage = [pltpu.VMEM((tokens, width), BF16)] * 2 + [pltpu.SemaphoreType.DMA((2 * nb,))]
    big = 2 * tokens * heads * e * BLK
    small = 2 * tokens * heads * e * e

    state, prefix, factors, q, k, v, cot = call(
        functools.partial(states_kernel, dims), "states",
        (decay_code, bnd, queries, keys, values, cotangent),
        (payload, local, ((len(ROWS) * up8(nb * heads), BLK), F32), narrow, narrow, narrow, narrow), small,
        hbm_in=True,
        scratch=(pltpu.SMEM((heads,), jnp.int32), pltpu.VMEM(bnd.shape, jnp.int32), pltpu.SemaphoreType.DMA((6,))),
    )
    masks, states, (weights, within, growth, beyond) = gather_states(state, lambda: call(
        functools.partial(within_kernel, dims), "within", (factors, q, k, v),
        (((nb, heads, BLK, BLK), BF16), wide, wide, wide), 2 * big,
    ))
    held, attended, sums = call(
        functools.partial(attend_kernel, dims, masks), "attend",
        (factors, q, cot, within, growth, prefix, *states),
        (((nb, heads, e, e), BF16), wide, ((up8(2 * nb), BLK), F32)), small,
    )
    sums = sum_over_heads(sums)
    grad, scale, grad_state, suffix = call(
        functools.partial(grad_kernel, dims, full_width, len(sums)), "grad",
        (factors, q, cot, attended, *sums),
        (narrow, ((up8(2 * nb), BLK), F32), payload, local), small,
    )
    masks, grad_states, (output, grad_queries, gk_part, gv_part) = gather_states(grad_state, lambda: call(
        functools.partial(inner_grads_kernel, dims), "inner_grads",
        (factors, q, k, v, grad, weights, held, attended, growth, scale),
        (narrow, narrow, wide, wide), 4 * big + small, hbm_outs=2, scratch=stage,
    ))
    grad_keys, grad_values = call(
        functools.partial(outer_grads_kernel, dims, masks), "outer_grads",
        (factors, k, v, gk_part, gv_part, beyond, suffix, *grad_states),
        (narrow, narrow), 2 * small, hbm_outs=2, scratch=stage,
    )
    return output, grad_queries, grad_keys, grad_values


def solution(mesh):
    both = P("ctx", "head")
    return jax.shard_map(
        shards,
        mesh=mesh,
        in_specs=(both, both, both, both, P("head"), P("ctx")),
        out_specs=(both, both, both, both),
        check_vma=False,
    )
```

```python
import functools
import math

import jax
import jax.numpy as jnp
from jax import lax
from jax.experimental import pallas as pl
from jax.experimental.pallas import tpu as pltpu
from jax.sharding import PartitionSpec as P

BLK = 256
LANES = 128
LOG_TWO = math.log(2.0)
EPSILON = 1e-06
F32 = jnp.float32
BF16 = jnp.bfloat16

NN = (((1,), (0,)), ((), ()))
NT = (((1,), (1,)), ((), ()))
TN = (((0,), (0,)), ((), ()))


def mm(a, b, dims=NN):
    return lax.dot_general(a, b, dims, preferred_element_type=F32)


def iota(shape, axis):
    return lax.broadcasted_iota(jnp.int32, shape, axis)


def up8(n):
    return -(-n // 8) * 8


def halves(x):
    head = x.astype(BF16)
    return head, (x - head.astype(F32)).astype(BF16)


ROWS = ("growth", "beyond", "decay", "total", "count", "rate")


def factor_rows(bnd_ref, code_ref, blocks, heads):
    rows = up8(blocks * heads)
    per = BLK // LANES
    bnd = bnd_ref[...].astype(F32)
    parts = []
    for b in range(blocks):
        row = jnp.concatenate([bnd[b * per + i : b * per + i + 1] for i in range(per)], axis=1)
        parts += [row] * heads
    if rows > blocks * heads:
        parts.append(jnp.zeros((rows - blocks * heads, BLK), F32))
    marks = jnp.concatenate(parts, axis=0).astype(BF16)
    upper = (iota((BLK, BLK), 0) <= iota((BLK, BLK), 1)).astype(F32).astype(BF16)
    count = mm(marks, upper)
    count_all = mm(marks, jnp.ones((BLK, BLK), BF16))
    which = iota((rows, BLK), 0)
    code = jnp.zeros((rows, BLK), F32)
    for h in range(heads):
        code = jnp.where(which % heads == h, code_ref[h].astype(F32), code)
    rate = jnp.log1p(code * -(2.0 ** (-20)))
    place = (iota((rows, BLK), 1) + 1).astype(F32)
    level = rate * place - LOG_TWO * count
    total = rate * float(BLK) - LOG_TWO * count_all
    return jnp.exp(level), jnp.exp(total - level), jnp.exp(total), total, count, rate


class Factors:
    def __init__(self, ref, blocks, heads):
        self.ref, self.blocks, self.heads, self.rows = ref, blocks, heads, up8(blocks * heads)

    def all(self, name):
        at = ROWS.index(name) * self.rows
        return self.ref[at : at + self.rows, :]

    def row(self, name, b, h, lanes=BLK):
        at = ROWS.index(name) * self.rows + b * self.heads + h
        return self.ref[at : at + 1, :lanes]

    def device_total(self, h):
        return sum(self.row("total", b, h, LANES) for b in range(self.blocks))

    def decays(self, b):
        pick = (iota((self.rows, BLK), 0) == b * self.heads).astype(F32).astype(BF16)
        count_i = mm(self.all("count").astype(BF16), pick, TN)
        halved = LOG_TWO * (count_i - self.row("count", b, 0))
        apart = iota((BLK, BLK), 0) - iota((BLK, BLK), 1)
        causal = apart >= 0
        steps = apart.astype(F32)
        return causal, [
            jnp.exp(jnp.where(causal, self.row("rate", b, h) * steps - halved, 0.0))
            for h in range(self.heads)
        ]


def spread(a, wanted, width):
    head, rest = halves(a)
    both = jnp.concatenate([head.astype(F32), rest.astype(F32)], axis=0).T.astype(BF16)
    rows = a.shape[0]
    result = []
    for some in wanted:
        lane, row = iota((2 * rows, width), 1), iota((2 * rows, width), 0) % rows
        pick = jnp.zeros((2 * rows, width), F32)
        for i, r in enumerate(some):
            share = lane // (width // len(some)) == i
            pick = jnp.where(jnp.logical_and(share, row == r), 1.0, pick)
        result.append(mm(both, pick.astype(BF16)))
    return result


def incoming(payloads, place, masks, h, head_size, heads, reverse):
    at = heads * head_size + h
    totals = [p[at : at + 1, :] for p in payloads]
    sources = [place ^ m for m in masks]

    def before(a, b):
        return a > b if reverse else a < b

    result = jnp.zeros((head_size, head_size), F32)
    for i, m in enumerate(masks):
        if m == 0:
            continue
        inner = jnp.zeros_like(totals[0])
        for j, other in enumerate(masks):
            if other in (0, m):
                continue
            between = jnp.logical_and(before(sources[i], sources[j]), before(sources[j], place))
            inner = inner + jnp.where(between, totals[j], 0.0)
        weight = jnp.where(before(sources[i], place), jnp.exp(inner), 0.0)
        result = result + weight * payloads[i][h * head_size : (h + 1) * head_size, :]
    return result


def store_totals(payload_ref, fac, head_size):
    rest = [fac.device_total(h) for h in range(fac.heads)]
    pad = up8(fac.heads) - fac.heads
    if pad:
        rest.append(jnp.zeros((pad, LANES), F32))
    payload_ref[fac.heads * head_size :, :] = jnp.concatenate(rest, axis=0)


def block(ref, b, h, e):
    return ref[b * BLK : (b + 1) * BLK, h * e : (h + 1) * e]


def states_kernel(
    dims, code_in, bnd_in, k_in, v_in,
    payload_ref, local_ref, factors_ref, k_ref, v_ref, code_ref, bnd_ref, sems,
):
    nb, heads, e = dims
    fetch = [
        pltpu.make_async_copy(s, d, sems.at[i])
        for i, (s, d) in enumerate(((code_in, code_ref), (bnd_in, bnd_ref)))
    ]
    for s, d in ((k_in, k_ref), (v_in, v_ref)):
        fetch.append(pltpu.make_async_copy(s, d, sems.at[len(fetch)]))
    for c in fetch:
        c.start()
    fetch[0].wait()
    fetch[1].wait()
    made = factor_rows(bnd_ref, code_ref, nb, heads)
    rows = up8(nb * heads)
    for i, a in enumerate(made):
        factors_ref[i * rows : (i + 1) * rows, :] = a
    fac = Factors(factors_ref, nb, heads)
    store_totals(payload_ref, fac, e)
    fetch[2].wait()
    fetch[3].wait()
    for h in range(heads):
        running = None
        for b in range(nb):
            scaled = (block(k_ref, b, h, e).T.astype(F32) * fac.row("beyond", b, h)).astype(BF16)
            term = mm(scaled, block(v_ref, b, h, e))
            running = term if running is None else fac.row("decay", b, h, e) * running + term
            if b < nb - 1:
                local_ref[b, h] = running
        payload_ref[h * e : (h + 1) * e, :] = running


def within_kernel(
    dims, q_in, cot_in, factors_ref, k_ref, v_ref,
    w_ref, within_ref, growth_ref, beyond_ref, lifted_ref, q_ref, cot_ref, sems,
):
    nb, heads, e = dims
    fetch = [
        pltpu.make_async_copy(s, d, sems.at[i])
        for i, (s, d) in enumerate(((q_in, q_ref), (cot_in, cot_ref)))
    ]
    for c in fetch:
        c.start()
    fac = Factors(factors_ref, nb, heads)
    wanted = [[b * heads + h for h in range(heads)] for b in range(nb)]
    for name, ref in (("growth", growth_ref), ("beyond", beyond_ref)):
        for b, a in enumerate(spread(fac.all(name), wanted, heads * e)):
            ref[b * BLK : (b + 1) * BLK, :] = a
    fetch[0].wait()
    for b in range(nb):
        causal, decays = fac.decays(b)
        for h in range(heads):
            q = block(q_ref, b, h, e)
            scores = mm(q, block(k_ref, b, h, e), NT)
            weights = jnp.where(causal, scores * decays[h], 0.0).astype(BF16)
            w_ref[b, h] = weights
            within_ref[b * BLK : (b + 1) * BLK, h * e : (h + 1) * e] = mm(
                weights, block(v_ref, b, h, e)
            )
            lifted_ref[b, h] = (q.T.astype(F32) * fac.row("growth", b, h)).astype(BF16)
    fetch[1].wait()


def row_sums(a):
    width = a.shape[1]
    narrow = sum(a[:, i : i + LANES] for i in range(0, width, LANES))
    return jnp.sum(narrow.T, axis=0, keepdims=True)


def attend_kernel(
    dims, masks, factors_ref, q_ref, cot_ref, within_ref, growth_ref, local_ref, *refs
):
    payloads, (held_ref, att_ref, sums_ref) = refs[: len(masks)], refs[len(masks) :]
    nb, heads, e = dims
    fac = Factors(factors_ref, nb, heads)
    for h in range(heads):
        arrived = incoming(payloads, lax.axis_index("ctx"), masks, h, e, heads, False)
        ahead = jnp.zeros((1, e), F32)
        for b in range(nb):
            state = jnp.exp(ahead) * arrived
            if b:
                state = state + local_ref[b - 1, h]
            ahead = ahead + fac.row("total", b, h, e)
            held_ref[b, h] = state.astype(BF16)
    squares, crosses = [], []
    for b in range(nb):
        rows = slice(b * BLK, (b + 1) * BLK)
        carried = jnp.concatenate(
            [mm(block(q_ref, b, h, e), held_ref[b, h]) for h in range(heads)], axis=1
        )
        att = within_ref[rows, :] + growth_ref[rows, :] * carried
        att_ref[rows, :] = att
        squares.append(row_sums(att * att))
        crosses.append(row_sums(att * cot_ref[rows, :].astype(F32)))
    parts = squares + crosses
    if up8(2 * nb) > 2 * nb:
        parts.append(jnp.zeros((up8(2 * nb) - 2 * nb, BLK), F32))
    sums_ref[...] = jnp.concatenate(parts, axis=0)


def grad_kernel(dims, full_width, parts, factors_ref, lifted_ref, cot_ref, att_ref, *refs):
    sums_refs, (g_ref, scale_ref, payload_ref, local_ref) = refs[:parts], refs[parts:]
    nb, heads, e = dims
    fac = Factors(factors_ref, nb, heads)
    sums = sum(ref[...] for ref in sums_refs)
    squares = jnp.where(iota(sums.shape, 0) < nb, sums, 0.0)
    scale = lax.rsqrt(squares / full_width + EPSILON)
    scale_ref[...] = scale
    squared = scale * scale
    lean = jnp.concatenate([squared[:nb], squared[:nb], squared[2 * nb :]], axis=0) * sums / full_width
    factors = jnp.where(iota(sums.shape, 0) < nb, scale, lean)
    columns = spread(factors, [[r] for r in range(2 * nb)], heads * e)
    for b in range(nb):
        rows = slice(b * BLK, (b + 1) * BLK)
        g_ref[rows, :] = (
            columns[b] * (cot_ref[rows, :].astype(F32) - att_ref[rows, :] * columns[nb + b])
        ).astype(BF16)
    for h in range(heads):
        running = None
        for b in reversed(range(nb)):
            term = mm(lifted_ref[b, h], block(g_ref, b, h, e))
            running = term if running is None else fac.row("decay", b, h, e) * running + term
            if b:
                local_ref[b - 1, h] = running
        payload_ref[h * e : (h + 1) * e, :] = running
    store_totals(payload_ref, fac, e)


def inner_grads_kernel(
    dims, factors_ref, q_ref, k_ref, v_ref, g_ref, w_ref, held_ref, att_ref, growth_ref, scale_ref,
    out_hbm, gq_hbm, gk_ref, gv_ref, out_ref, gq_ref, sems,
):
    nb, heads, e = dims
    fac = Factors(factors_ref, nb, heads)
    scale = spread(scale_ref[...], [[b] for b in range(nb)], heads * e)
    copies = []
    for b in range(nb):
        rows = slice(b * BLK, (b + 1) * BLK)
        out_ref[rows, :] = (att_ref[rows, :] * scale[b]).astype(BF16)
        copies.append(
            pltpu.make_async_copy(out_ref.at[rows], out_hbm.at[rows], sems.at[2 * b])
        )
        copies[-1].start()
        causal, decays = fac.decays(b)
        for h in range(heads):
            cols = slice(h * e, (h + 1) * e)
            g = block(g_ref, b, h, e)
            scores = mm(g, block(v_ref, b, h, e), NT)
            gw = jnp.where(causal, scores * decays[h], 0.0).astype(BF16)
            gq = mm(gw, block(k_ref, b, h, e)) + growth_ref[rows, cols] * mm(g, held_ref[b, h], NT)
            gq_ref[rows, cols] = gq.astype(BF16)
            gk_ref[rows, cols] = mm(gw, block(q_ref, b, h, e), TN)
            gv_ref[rows, cols] = mm(w_ref[b, h], g, TN)
        copies.append(
            pltpu.make_async_copy(gq_ref.at[rows], gq_hbm.at[rows], sems.at[2 * b + 1])
        )
        copies[-1].start()
    for c in copies:
        c.wait()


def outer_grads_kernel(
    dims, masks, factors_ref, k_ref, v_ref, gk_part_ref, gv_part_ref, beyond_ref, local_ref, *refs
):
    payloads, (gk_hbm, gv_hbm, gk_ref, gv_ref, sems) = refs[: len(masks)], refs[len(masks) :]
    nb, heads, e = dims
    fac = Factors(factors_ref, nb, heads)
    arrived = [incoming(payloads, lax.axis_index("ctx"), masks, h, e, heads, True) for h in range(heads)]
    behind = [jnp.zeros((1, e), F32) for h in range(heads)]
    copies = []
    for b in reversed(range(nb)):
        rows = slice(b * BLK, (b + 1) * BLK)
        for h in range(heads):
            cols = slice(h * e, (h + 1) * e)
            state = jnp.exp(behind[h]) * arrived[h]
            if b < nb - 1:
                state = state + local_ref[b, h]
            behind[h] = behind[h] + fac.row("total", b, h, e)
            held = state.astype(BF16)
            far = beyond_ref[rows, cols]
            gk = gk_part_ref[rows, cols] + far * mm(block(v_ref, b, h, e), held, NT)
            gk_ref[rows, cols] = gk.astype(BF16)
            gv = gv_part_ref[rows, cols] + far * mm(block(k_ref, b, h, e), held)
            gv_ref[rows, cols] = gv.astype(BF16)
        for i, (s, d) in enumerate(((gk_ref, gk_hbm), (gv_ref, gv_hbm))):
            copies.append(pltpu.make_async_copy(s.at[rows], d.at[rows], sems.at[2 * b + i]))
            copies[-1].start()
    for c in copies:
        c.wait()


def call(kernel, name, args, outs, flops, hbm_ins=0, hbm_outs=0, scratch=()):
    traffic = sum(a.size * a.dtype.itemsize for a in args) + sum(
        math.prod(s) * jnp.dtype(d).itemsize for s, d in outs
    )
    hbm = pl.BlockSpec(memory_space=pltpu.HBM)
    vmem = pl.BlockSpec(memory_space=pltpu.VMEM)
    args = [
        pltpu.with_memory_space_constraint(a, pltpu.HBM) if i < hbm_ins else a for i, a in enumerate(args)
    ]
    return pl.pallas_call(
        kernel,
        out_shape=[(pltpu.HBM if i < hbm_outs else pltpu.VMEM)(s, d) for i, (s, d) in enumerate(outs)],
        in_specs=[hbm if i < hbm_ins else vmem for i in range(len(args))],
        out_specs=[hbm if i < hbm_outs else vmem for i in range(len(outs))],
        scratch_shapes=scratch,
        compiler_params=pltpu.CompilerParams(vmem_limit_bytes=16 * 2**20),
        cost_estimate=pl.CostEstimate(flops=flops, bytes_accessed=traffic, transcendentals=0),
        name=name,
    )(*args)


def nothing(*refs):
    pass


def after(a, other):
    anywhere = pl.BlockSpec(memory_space=pltpu.VMEM)
    return pl.pallas_call(
        nothing,
        out_shape=pltpu.VMEM(a.shape, a.dtype),
        in_specs=[anywhere, anywhere],
        out_specs=anywhere,
        input_output_aliases={0: 0},
        compiler_params=pltpu.CompilerParams(vmem_limit_bytes=4 * 2**20),
        name="after",
    )(a, other)


def swap(a, axis, mask):
    return lax.ppermute(a, axis, [(i, i ^ mask) for i in range(lax.axis_size(axis))])


def gather_states(payload, work):
    bit = lax.axis_size("ctx") // 2
    first = swap(payload, "ctx", bit) if bit else payload
    done = work()
    first = after(first, done[-1])
    masks, held = ([0, bit], [payload, first]) if bit else ([0], [payload])
    bit //= 2
    while bit:
        held += [swap(a, "ctx", bit) for a in held]
        masks += [m | bit for m in masks]
        bit //= 2
    return masks, held, done


def sum_over_heads(sums):
    size = lax.axis_size("head")
    rounds = [range(1, min(4, size))] + [[bit] for bit in (4, 8, 16, 32, 64, 128) if bit < size]
    parts = [sums]
    for apart in rounds:
        own = functools.reduce(jnp.add, parts)
        parts = [own] + [swap(own, "head", k) for k in apart]
    return parts


def shards(queries, keys, values, cotangent, decay_code, boundaries):
    tokens, width = queries.shape
    heads = decay_code.shape[0]
    e = width // heads
    nb = tokens // BLK
    dims = (nb, heads, e)
    full_width = width * lax.axis_size("head")
    bnd = boundaries.reshape(tokens // LANES, LANES)
    payload = ((heads * e + up8(heads), LANES), F32)
    local = ((max(nb - 1, 1), heads, e, e), F32)
    narrow, wide = ((tokens, width), BF16), ((tokens, width), F32)
    stage = [pltpu.VMEM((tokens, width), BF16)] * 2 + [pltpu.SemaphoreType.DMA((2 * nb,))]
    big = 2 * tokens * heads * e * BLK
    small = 2 * tokens * heads * e * e

    state, prefix, factors, k, v = call(
        functools.partial(states_kernel, dims), "states", (decay_code, bnd, keys, values),
        (payload, local, ((len(ROWS) * up8(nb * heads), BLK), F32), narrow, narrow), small, hbm_ins=4,
        scratch=(pltpu.SMEM((heads,), jnp.int32), pltpu.VMEM(bnd.shape, jnp.int32), pltpu.SemaphoreType.DMA((4,))),
    )
    masks, states, (weights, within, growth, beyond, lifted, q, cot) = gather_states(state, lambda: call(
        functools.partial(within_kernel, dims), "within", (queries, cotangent, factors, k, v),
        (((nb, heads, BLK, BLK), BF16), wide, wide, wide, ((nb, heads, e, BLK), BF16), narrow, narrow), 2 * big,
        hbm_ins=2, scratch=(pltpu.SemaphoreType.DMA((2,)),),
    ))
    held, attended, sums = call(
        functools.partial(attend_kernel, dims, masks), "attend",
        (factors, q, cot, within, growth, prefix, *states),
        (((nb, heads, e, e), BF16), wide, ((up8(2 * nb), BLK), F32)), small,
    )
    sums = sum_over_heads(sums)
    grad, scale, grad_state, suffix = call(
        functools.partial(grad_kernel, dims, full_width, len(sums)), "grad",
        (factors, lifted, cot, attended, *sums),
        (narrow, ((up8(2 * nb), BLK), F32), payload, local), small,
    )
    masks, grad_states, (output, grad_queries, gk_part, gv_part) = gather_states(grad_state, lambda: call(
        functools.partial(inner_grads_kernel, dims), "inner_grads",
        (factors, q, k, v, grad, weights, held, attended, growth, scale),
        (narrow, narrow, wide, wide), 4 * big + small, hbm_outs=2, scratch=stage,
    ))
    grad_keys, grad_values = call(
        functools.partial(outer_grads_kernel, dims, masks), "outer_grads",
        (factors, k, v, gk_part, gv_part, beyond, suffix, *grad_states),
        (narrow, narrow), 2 * small, hbm_outs=2, scratch=stage,
    )
    return output, grad_queries, grad_keys, grad_values


def solution(mesh):
    both = P("ctx", "head")
    return jax.shard_map(
        shards,
        mesh=mesh,
        in_specs=(both, both, both, both, P("head"), P("ctx")),
        out_specs=(both, both, both, both),
        check_vma=False,
    )
```

```python
import functools
import math

import jax
import jax.numpy as jnp
from jax import lax
from jax.experimental import pallas as pl
from jax.experimental.pallas import tpu as pltpu
from jax.sharding import PartitionSpec as P

BLK = 256
LANES = 128
LOG_TWO = math.log(2.0)
EPSILON = 1e-06
F32 = jnp.float32
BF16 = jnp.bfloat16

NN = (((1,), (0,)), ((), ()))
NT = (((1,), (1,)), ((), ()))
TN = (((0,), (0,)), ((), ()))


def mm(a, b, dims=NN):
    return lax.dot_general(a, b, dims, preferred_element_type=F32)


def iota(shape, axis):
    return lax.broadcasted_iota(jnp.int32, shape, axis)


def up8(n):
    return -(-n // 8) * 8


def halves(x):
    head = x.astype(BF16)
    return head, (x - head.astype(F32)).astype(BF16)


ROWS = ("growth", "beyond", "decay", "total", "count", "rate")


def factor_rows(bnd_ref, code_ref, blocks, heads):
    rows = up8(blocks * heads)
    per = BLK // LANES
    bnd = bnd_ref[...].astype(F32)
    parts = []
    for b in range(blocks):
        row = jnp.concatenate([bnd[b * per + i : b * per + i + 1] for i in range(per)], axis=1)
        parts += [row] * heads
    if rows > blocks * heads:
        parts.append(jnp.zeros((rows - blocks * heads, BLK), F32))
    marks = jnp.concatenate(parts, axis=0).astype(BF16)
    upper = (iota((BLK, BLK), 0) <= iota((BLK, BLK), 1)).astype(F32).astype(BF16)
    count = mm(marks, upper)
    count_all = mm(marks, jnp.ones((BLK, BLK), BF16))
    which = iota((rows, BLK), 0)
    code = jnp.zeros((rows, BLK), F32)
    for h in range(heads):
        code = jnp.where(which % heads == h, code_ref[h].astype(F32), code)
    rate = jnp.log1p(code * -(2.0 ** (-20)))
    place = (iota((rows, BLK), 1) + 1).astype(F32)
    level = rate * place - LOG_TWO * count
    total = rate * float(BLK) - LOG_TWO * count_all
    return jnp.exp(level), jnp.exp(total - level), jnp.exp(total), total, count, rate


class Factors:
    def __init__(self, ref, blocks, heads):
        self.ref, self.blocks, self.heads, self.rows = ref, blocks, heads, up8(blocks * heads)

    def all(self, name):
        at = ROWS.index(name) * self.rows
        return self.ref[at : at + self.rows, :]

    def row(self, name, b, h, lanes=BLK):
        at = ROWS.index(name) * self.rows + b * self.heads + h
        return self.ref[at : at + 1, :lanes]

    def device_total(self, h):
        return sum(self.row("total", b, h, LANES) for b in range(self.blocks))

    def decays(self, b):
        pick = (iota((self.rows, BLK), 0) == b * self.heads).astype(F32).astype(BF16)
        count_i = mm(self.all("count").astype(BF16), pick, TN)
        halved = LOG_TWO * (count_i - self.row("count", b, 0))
        apart = iota((BLK, BLK), 0) - iota((BLK, BLK), 1)
        causal = apart >= 0
        steps = apart.astype(F32)
        return causal, [
            jnp.exp(jnp.where(causal, self.row("rate", b, h) * steps - halved, 0.0))
            for h in range(self.heads)
        ]


def spread(a, wanted, width):
    head, rest = halves(a)
    both = jnp.concatenate([head.astype(F32), rest.astype(F32)], axis=0).T.astype(BF16)
    rows = a.shape[0]
    result = []
    for some in wanted:
        lane, row = iota((2 * rows, width), 1), iota((2 * rows, width), 0) % rows
        pick = jnp.zeros((2 * rows, width), F32)
        for i, r in enumerate(some):
            share = lane // (width // len(some)) == i
            pick = jnp.where(jnp.logical_and(share, row == r), 1.0, pick)
        result.append(mm(both, pick.astype(BF16)))
    return result


def incoming(payloads, place, masks, h, head_size, heads, reverse):
    at = heads * head_size + h
    totals = [p[at : at + 1, :] for p in payloads]
    sources = [place ^ m for m in masks]

    def before(a, b):
        return a > b if reverse else a < b

    result = jnp.zeros((head_size, head_size), F32)
    for i, m in enumerate(masks):
        if m == 0:
            continue
        inner = jnp.zeros_like(totals[0])
        for j, other in enumerate(masks):
            if other in (0, m):
                continue
            between = jnp.logical_and(before(sources[i], sources[j]), before(sources[j], place))
            inner = inner + jnp.where(between, totals[j], 0.0)
        weight = jnp.where(before(sources[i], place), jnp.exp(inner), 0.0)
        result = result + weight * payloads[i][h * head_size : (h + 1) * head_size, :]
    return result


def store_totals(payload_ref, fac, head_size):
    rest = [fac.device_total(h) for h in range(fac.heads)]
    pad = up8(fac.heads) - fac.heads
    if pad:
        rest.append(jnp.zeros((pad, LANES), F32))
    payload_ref[fac.heads * head_size :, :] = jnp.concatenate(rest, axis=0)


def block(ref, b, h, e):
    return ref[b * BLK : (b + 1) * BLK, h * e : (h + 1) * e]


def states_kernel(
    dims, code_in, bnd_in, k_in, v_in,
    payload_ref, local_ref, factors_ref, k_ref, v_ref, code_ref, bnd_ref, sems,
):
    nb, heads, e = dims
    fetch = [
        pltpu.make_async_copy(s, d, sems.at[i])
        for i, (s, d) in enumerate(((code_in, code_ref), (bnd_in, bnd_ref)))
    ]
    for s, d in ((k_in, k_ref), (v_in, v_ref)):
        fetch.append(pltpu.make_async_copy(s, d, sems.at[len(fetch)]))
    for c in fetch:
        c.start()
    fetch[0].wait()
    fetch[1].wait()
    made = factor_rows(bnd_ref, code_ref, nb, heads)
    rows = up8(nb * heads)
    for i, a in enumerate(made):
        factors_ref[i * rows : (i + 1) * rows, :] = a
    fac = Factors(factors_ref, nb, heads)
    store_totals(payload_ref, fac, e)
    fetch[2].wait()
    fetch[3].wait()
    for h in range(heads):
        running = None
        for b in range(nb):
            scaled = (block(k_ref, b, h, e).T.astype(F32) * fac.row("beyond", b, h)).astype(BF16)
            term = mm(scaled, block(v_ref, b, h, e))
            running = term if running is None else fac.row("decay", b, h, e) * running + term
            if b < nb - 1:
                local_ref[b, h] = running
        payload_ref[h * e : (h + 1) * e, :] = running


def within_kernel(
    dims, q_in, cot_in, factors_ref, k_ref, v_ref,
    w_ref, within_ref, growth_ref, beyond_ref, lifted_ref, q_ref, cot_ref, sems,
):
    nb, heads, e = dims
    fetch = [
        pltpu.make_async_copy(s, d, sems.at[i])
        for i, (s, d) in enumerate(((q_in, q_ref), (cot_in, cot_ref)))
    ]
    for c in fetch:
        c.start()
    fac = Factors(factors_ref, nb, heads)
    wanted = [[b * heads + h for h in range(heads)] for b in range(nb)]
    for name, ref in (("growth", growth_ref), ("beyond", beyond_ref)):
        for b, a in enumerate(spread(fac.all(name), wanted, heads * e)):
            ref[b * BLK : (b + 1) * BLK, :] = a
    fetch[0].wait()
    for b in range(nb):
        causal, decays = fac.decays(b)
        for h in range(heads):
            q = block(q_ref, b, h, e)
            scores = mm(q, block(k_ref, b, h, e), NT)
            weights = jnp.where(causal, scores * decays[h], 0.0).astype(BF16)
            w_ref[b, h] = weights
            within_ref[b * BLK : (b + 1) * BLK, h * e : (h + 1) * e] = mm(
                weights, block(v_ref, b, h, e)
            )
            lifted_ref[b, h] = (q.T.astype(F32) * fac.row("growth", b, h)).astype(BF16)
    fetch[1].wait()


def row_sums(a):
    width = a.shape[1]
    narrow = sum(a[:, i : i + LANES] for i in range(0, width, LANES))
    return jnp.sum(narrow.T, axis=0, keepdims=True)


def attend_kernel(
    dims, masks, factors_ref, q_ref, cot_ref, within_ref, growth_ref, local_ref, *refs
):
    payloads, (held_ref, att_ref, sums_ref) = refs[: len(masks)], refs[len(masks) :]
    nb, heads, e = dims
    fac = Factors(factors_ref, nb, heads)
    for h in range(heads):
        arrived = incoming(payloads, lax.axis_index("ctx"), masks, h, e, heads, False)
        ahead = jnp.zeros((1, e), F32)
        for b in range(nb):
            state = jnp.exp(ahead) * arrived
            if b:
                state = state + local_ref[b - 1, h]
            ahead = ahead + fac.row("total", b, h, e)
            held_ref[b, h] = state.astype(BF16)
    squares, crosses = [], []
    for b in range(nb):
        rows = slice(b * BLK, (b + 1) * BLK)
        carried = jnp.concatenate(
            [mm(block(q_ref, b, h, e), held_ref[b, h]) for h in range(heads)], axis=1
        )
        att = within_ref[rows, :] + growth_ref[rows, :] * carried
        att_ref[rows, :] = att
        squares.append(row_sums(att * att))
        crosses.append(row_sums(att * cot_ref[rows, :].astype(F32)))
    parts = squares + crosses
    if up8(2 * nb) > 2 * nb:
        parts.append(jnp.zeros((up8(2 * nb) - 2 * nb, BLK), F32))
    sums_ref[...] = jnp.concatenate(parts, axis=0)


def grad_kernel(dims, full_width, parts, factors_ref, lifted_ref, cot_ref, att_ref, *refs):
    sums_refs, (g_ref, scale_ref, payload_ref, local_ref) = refs[:parts], refs[parts:]
    nb, heads, e = dims
    fac = Factors(factors_ref, nb, heads)
    sums = sum(ref[...] for ref in sums_refs)
    squares = jnp.where(iota(sums.shape, 0) < nb, sums, 0.0)
    scale = lax.rsqrt(squares / full_width + EPSILON)
    scale_ref[...] = scale
    squared = scale * scale
    lean = jnp.concatenate([squared[:nb], squared[:nb], squared[2 * nb :]], axis=0) * sums / full_width
    factors = jnp.where(iota(sums.shape, 0) < nb, scale, lean)
    columns = spread(factors, [[r] for r in range(2 * nb)], e)
    running = [None] * heads
    for b in reversed(range(nb)):
        rows = slice(b * BLK, (b + 1) * BLK)
        for h in range(heads):
            cols = slice(h * e, (h + 1) * e)
            g = columns[b] * (cot_ref[rows, cols].astype(F32) - att_ref[rows, cols] * columns[nb + b])
            g = g.astype(BF16)
            g_ref[rows, cols] = g
            term = mm(lifted_ref[b, h], g)
            running[h] = term if b == nb - 1 else fac.row("decay", b, h, e) * running[h] + term
            if b:
                local_ref[b - 1, h] = running[h]
    for h in range(heads):
        payload_ref[h * e : (h + 1) * e, :] = running[h]
    store_totals(payload_ref, fac, e)


def inner_grads_kernel(
    dims, factors_ref, q_ref, k_ref, v_ref, g_ref, w_ref, held_ref, att_ref, growth_ref, scale_ref,
    out_hbm, gq_hbm, gk_ref, gv_ref, out_ref, gq_ref, sems,
):
    nb, heads, e = dims
    fac = Factors(factors_ref, nb, heads)
    scale = spread(scale_ref[...], [[b] for b in range(nb)], heads * e)
    copies = []
    for b in range(nb):
        rows = slice(b * BLK, (b + 1) * BLK)
        out_ref[rows, :] = (att_ref[rows, :] * scale[b]).astype(BF16)
        copies.append(
            pltpu.make_async_copy(out_ref.at[rows], out_hbm.at[rows], sems.at[2 * b])
        )
        copies[-1].start()
        causal, decays = fac.decays(b)
        for h in range(heads):
            cols = slice(h * e, (h + 1) * e)
            g = block(g_ref, b, h, e)
            scores = mm(g, block(v_ref, b, h, e), NT)
            gw = jnp.where(causal, scores * decays[h], 0.0).astype(BF16)
            gq = mm(gw, block(k_ref, b, h, e)) + growth_ref[rows, cols] * mm(g, held_ref[b, h], NT)
            gq_ref[rows, cols] = gq.astype(BF16)
            gk_ref[rows, cols] = mm(gw, block(q_ref, b, h, e), TN)
            gv_ref[rows, cols] = mm(w_ref[b, h], g, TN)
        copies.append(
            pltpu.make_async_copy(gq_ref.at[rows], gq_hbm.at[rows], sems.at[2 * b + 1])
        )
        copies[-1].start()
    for c in copies:
        c.wait()


def outer_grads_kernel(
    dims, masks, factors_ref, k_ref, v_ref, gk_part_ref, gv_part_ref, beyond_ref, local_ref, *refs
):
    payloads, (gk_hbm, gv_hbm, gk_ref, gv_ref, sems) = refs[: len(masks)], refs[len(masks) :]
    nb, heads, e = dims
    fac = Factors(factors_ref, nb, heads)
    arrived = [incoming(payloads, lax.axis_index("ctx"), masks, h, e, heads, True) for h in range(heads)]
    behind = [jnp.zeros((1, e), F32) for h in range(heads)]
    copies = []
    for b in reversed(range(nb)):
        rows = slice(b * BLK, (b + 1) * BLK)
        for h in range(heads):
            cols = slice(h * e, (h + 1) * e)
            state = jnp.exp(behind[h]) * arrived[h]
            if b < nb - 1:
                state = state + local_ref[b, h]
            behind[h] = behind[h] + fac.row("total", b, h, e)
            held = state.astype(BF16)
            far = beyond_ref[rows, cols]
            gk = gk_part_ref[rows, cols] + far * mm(block(v_ref, b, h, e), held, NT)
            gk_ref[rows, cols] = gk.astype(BF16)
            gv = gv_part_ref[rows, cols] + far * mm(block(k_ref, b, h, e), held)
            gv_ref[rows, cols] = gv.astype(BF16)
        for i, (s, d) in enumerate(((gk_ref, gk_hbm), (gv_ref, gv_hbm))):
            copies.append(pltpu.make_async_copy(s.at[rows], d.at[rows], sems.at[2 * b + i]))
            copies[-1].start()
    for c in copies:
        c.wait()


def call(kernel, name, args, outs, flops, hbm_ins=0, hbm_outs=0, scratch=()):
    traffic = sum(a.size * a.dtype.itemsize for a in args) + sum(
        math.prod(s) * jnp.dtype(d).itemsize for s, d in outs
    )
    hbm = pl.BlockSpec(memory_space=pltpu.HBM)
    vmem = pl.BlockSpec(memory_space=pltpu.VMEM)
    args = [
        pltpu.with_memory_space_constraint(a, pltpu.HBM) if i < hbm_ins else a for i, a in enumerate(args)
    ]
    return pl.pallas_call(
        kernel,
        out_shape=[(pltpu.HBM if i < hbm_outs else pltpu.VMEM)(s, d) for i, (s, d) in enumerate(outs)],
        in_specs=[hbm if i < hbm_ins else vmem for i in range(len(args))],
        out_specs=[hbm if i < hbm_outs else vmem for i in range(len(outs))],
        scratch_shapes=scratch,
        compiler_params=pltpu.CompilerParams(vmem_limit_bytes=16 * 2**20),
        cost_estimate=pl.CostEstimate(flops=flops, bytes_accessed=traffic, transcendentals=0),
        name=name,
    )(*args)


def nothing(*refs):
    pass


def after(a, other):
    anywhere = pl.BlockSpec(memory_space=pltpu.VMEM)
    return pl.pallas_call(
        nothing,
        out_shape=pltpu.VMEM(a.shape, a.dtype),
        in_specs=[anywhere, anywhere],
        out_specs=anywhere,
        input_output_aliases={0: 0},
        compiler_params=pltpu.CompilerParams(vmem_limit_bytes=4 * 2**20),
        name="after",
    )(a, other)


def swap(a, axis, mask):
    return lax.ppermute(a, axis, [(i, i ^ mask) for i in range(lax.axis_size(axis))])


def gather_states(payload, work):
    bit = lax.axis_size("ctx") // 2
    first = swap(payload, "ctx", bit) if bit else payload
    done = work()
    first = after(first, done[-1])
    masks, held = ([0, bit], [payload, first]) if bit else ([0], [payload])
    bit //= 2
    while bit:
        held += [swap(a, "ctx", bit) for a in held]
        masks += [m | bit for m in masks]
        bit //= 2
    return masks, held, done


def sum_over_heads(sums):
    size = lax.axis_size("head")
    rounds = [range(1, min(4, size))] + [[bit] for bit in (4, 8, 16, 32, 64, 128) if bit < size]
    parts = [sums]
    for apart in rounds:
        own = functools.reduce(jnp.add, parts)
        parts = [own] + [swap(own, "head", k) for k in apart]
    return parts


def shards(queries, keys, values, cotangent, decay_code, boundaries):
    tokens, width = queries.shape
    heads = decay_code.shape[0]
    e = width // heads
    nb = tokens // BLK
    dims = (nb, heads, e)
    full_width = width * lax.axis_size("head")
    bnd = boundaries.reshape(tokens // LANES, LANES)
    payload = ((heads * e + up8(heads), LANES), F32)
    local = ((max(nb - 1, 1), heads, e, e), F32)
    narrow, wide = ((tokens, width), BF16), ((tokens, width), F32)
    stage = [pltpu.VMEM((tokens, width), BF16)] * 2 + [pltpu.SemaphoreType.DMA((2 * nb,))]
    big = 2 * tokens * heads * e * BLK
    small = 2 * tokens * heads * e * e

    state, prefix, factors, k, v = call(
        functools.partial(states_kernel, dims), "states", (decay_code, bnd, keys, values),
        (payload, local, ((len(ROWS) * up8(nb * heads), BLK), F32), narrow, narrow), small, hbm_ins=4,
        scratch=(pltpu.SMEM((heads,), jnp.int32), pltpu.VMEM(bnd.shape, jnp.int32), pltpu.SemaphoreType.DMA((4,))),
    )
    masks, states, (weights, within, growth, beyond, lifted, q, cot) = gather_states(state, lambda: call(
        functools.partial(within_kernel, dims), "within", (queries, cotangent, factors, k, v),
        (((nb, heads, BLK, BLK), BF16), wide, wide, wide, ((nb, heads, e, BLK), BF16), narrow, narrow), 2 * big,
        hbm_ins=2, scratch=(pltpu.SemaphoreType.DMA((2,)),),
    ))
    held, attended, sums = call(
        functools.partial(attend_kernel, dims, masks), "attend",
        (factors, q, cot, within, growth, prefix, *states),
        (((nb, heads, e, e), BF16), wide, ((up8(2 * nb), BLK), F32)), small,
    )
    sums = sum_over_heads(sums)
    grad, scale, grad_state, suffix = call(
        functools.partial(grad_kernel, dims, full_width, len(sums)), "grad",
        (factors, lifted, cot, attended, *sums),
        (narrow, ((up8(2 * nb), BLK), F32), payload, local), small,
    )
    masks, grad_states, (output, grad_queries, gk_part, gv_part) = gather_states(grad_state, lambda: call(
        functools.partial(inner_grads_kernel, dims), "inner_grads",
        (factors, q, k, v, grad, weights, held, attended, growth, scale),
        (narrow, narrow, wide, wide), 4 * big + small, hbm_outs=2, scratch=stage,
    ))
    grad_keys, grad_values = call(
        functools.partial(outer_grads_kernel, dims, masks), "outer_grads",
        (factors, k, v, gk_part, gv_part, beyond, suffix, *grad_states),
        (narrow, narrow), 2 * small, hbm_outs=2, scratch=stage,
    )
    return output, grad_queries, grad_keys, grad_values


def solution(mesh):
    both = P("ctx", "head")
    return jax.shard_map(
        shards,
        mesh=mesh,
        in_specs=(both, both, both, both, P("head"), P("ctx")),
        out_specs=(both, both, both, both),
        check_vma=False,
    )
```

```python
import functools
import math

import jax
import jax.numpy as jnp
from jax import lax
from jax.experimental import pallas as pl
from jax.experimental.pallas import tpu as pltpu
from jax.sharding import PartitionSpec as P

BLK = 256
LANES = 128
LOG_TWO = math.log(2.0)
EPSILON = 1e-06
F32 = jnp.float32
BF16 = jnp.bfloat16

NN = (((1,), (0,)), ((), ()))
NT = (((1,), (1,)), ((), ()))
TN = (((0,), (0,)), ((), ()))


def mm(a, b, dims=NN):
    return lax.dot_general(a, b, dims, preferred_element_type=F32)


def iota(shape, axis):
    return lax.broadcasted_iota(jnp.int32, shape, axis)


def up8(n):
    return -(-n // 8) * 8


def halves(x):
    head = x.astype(BF16)
    return head, (x - head.astype(F32)).astype(BF16)


ROWS = ("growth", "beyond", "decay", "total", "count", "rate")


def factor_rows(bnd_ref, code_ref, blocks, heads):
    rows = up8(blocks * heads)
    per = BLK // LANES
    bnd = bnd_ref[...].astype(F32)
    parts = []
    for b in range(blocks):
        row = jnp.concatenate([bnd[b * per + i : b * per + i + 1] for i in range(per)], axis=1)
        parts += [row] * heads
    if rows > blocks * heads:
        parts.append(jnp.zeros((rows - blocks * heads, BLK), F32))
    marks = jnp.concatenate(parts, axis=0).astype(BF16)
    upper = (iota((BLK, BLK), 0) <= iota((BLK, BLK), 1)).astype(F32).astype(BF16)
    count = mm(marks, upper)
    count_all = mm(marks, jnp.ones((BLK, BLK), BF16))
    which = iota((rows, BLK), 0)
    code = jnp.zeros((rows, BLK), F32)
    for h in range(heads):
        code = jnp.where(which % heads == h, code_ref[h].astype(F32), code)
    rate = jnp.log1p(code * -(2.0 ** (-20)))
    place = (iota((rows, BLK), 1) + 1).astype(F32)
    level = rate * place - LOG_TWO * count
    total = rate * float(BLK) - LOG_TWO * count_all
    return jnp.exp(level), jnp.exp(total - level), jnp.exp(total), total, count, rate


class Factors:
    def __init__(self, ref, blocks, heads):
        self.ref, self.blocks, self.heads, self.rows = ref, blocks, heads, up8(blocks * heads)

    def all(self, name):
        at = ROWS.index(name) * self.rows
        return self.ref[at : at + self.rows, :]

    def row(self, name, b, h, lanes=BLK):
        at = ROWS.index(name) * self.rows + b * self.heads + h
        return self.ref[at : at + 1, :lanes]

    def device_total(self, h):
        return sum(self.row("total", b, h, LANES) for b in range(self.blocks))

    def decays(self, b):
        pick = (iota((self.rows, BLK), 0) == b * self.heads).astype(F32).astype(BF16)
        count_i = mm(self.all("count").astype(BF16), pick, TN)
        halved = LOG_TWO * (count_i - self.row("count", b, 0))
        apart = iota((BLK, BLK), 0) - iota((BLK, BLK), 1)
        causal = apart >= 0
        steps = apart.astype(F32)
        return causal, [
            jnp.exp(jnp.where(causal, self.row("rate", b, h) * steps - halved, 0.0))
            for h in range(self.heads)
        ]


def spread(a, wanted, width):
    head, rest = halves(a)
    both = jnp.concatenate([head.astype(F32), rest.astype(F32)], axis=0).T.astype(BF16)
    rows = a.shape[0]
    result = []
    for some in wanted:
        lane, row = iota((2 * rows, width), 1), iota((2 * rows, width), 0) % rows
        pick = jnp.zeros((2 * rows, width), F32)
        for i, r in enumerate(some):
            share = lane // (width // len(some)) == i
            pick = jnp.where(jnp.logical_and(share, row == r), 1.0, pick)
        result.append(mm(both, pick.astype(BF16)))
    return result


def incoming(payloads, place, masks, h, head_size, heads, reverse):
    at = heads * head_size + h
    totals = [p[at : at + 1, :] for p in payloads]
    sources = [place ^ m for m in masks]

    def before(a, b):
        return a > b if reverse else a < b

    result = jnp.zeros((head_size, head_size), F32)
    for i, m in enumerate(masks):
        if m == 0:
            continue
        inner = jnp.zeros_like(totals[0])
        for j, other in enumerate(masks):
            if other in (0, m):
                continue
            between = jnp.logical_and(before(sources[i], sources[j]), before(sources[j], place))
            inner = inner + jnp.where(between, totals[j], 0.0)
        weight = jnp.where(before(sources[i], place), jnp.exp(inner), 0.0)
        result = result + weight * payloads[i][h * head_size : (h + 1) * head_size, :]
    return result


def store_totals(payload_ref, fac, head_size):
    rest = [fac.device_total(h) for h in range(fac.heads)]
    pad = up8(fac.heads) - fac.heads
    if pad:
        rest.append(jnp.zeros((pad, LANES), F32))
    payload_ref[fac.heads * head_size :, :] = jnp.concatenate(rest, axis=0)


def block(ref, b, h, e):
    return ref[b * BLK : (b + 1) * BLK, h * e : (h + 1) * e]


def states_kernel(
    dims, code_in, bnd_in, k_in, v_in,
    payload_ref, local_ref, factors_ref, k_ref, v_ref, code_ref, bnd_ref, sems,
):
    nb, heads, e = dims
    fetch = [
        pltpu.make_async_copy(s, d, sems.at[i])
        for i, (s, d) in enumerate(((code_in, code_ref), (bnd_in, bnd_ref)))
    ]
    for s, d in ((k_in, k_ref), (v_in, v_ref)):
        fetch.append(pltpu.make_async_copy(s, d, sems.at[len(fetch)]))
    for c in fetch:
        c.start()
    fetch[0].wait()
    fetch[1].wait()
    made = factor_rows(bnd_ref, code_ref, nb, heads)
    rows = up8(nb * heads)
    for i, a in enumerate(made):
        factors_ref[i * rows : (i + 1) * rows, :] = a
    fac = Factors(factors_ref, nb, heads)
    store_totals(payload_ref, fac, e)
    fetch[2].wait()
    fetch[3].wait()
    for h in range(heads):
        running = None
        for b in range(nb):
            scaled = (block(k_ref, b, h, e).T.astype(F32) * fac.row("beyond", b, h)).astype(BF16)
            term = mm(scaled, block(v_ref, b, h, e))
            running = term if running is None else fac.row("decay", b, h, e) * running + term
            if b < nb - 1:
                local_ref[b, h] = running
        payload_ref[h * e : (h + 1) * e, :] = running


def within_kernel(
    dims, q_in, cot_in, factors_ref, k_ref, v_ref,
    w_ref, within_ref, growth_ref, beyond_ref, lifted_ref, q_ref, cot_ref, sems,
):
    nb, heads, e = dims
    fetch = [
        pltpu.make_async_copy(s, d, sems.at[i])
        for i, (s, d) in enumerate(((q_in, q_ref), (cot_in, cot_ref)))
    ]
    for c in fetch:
        c.start()
    fac = Factors(factors_ref, nb, heads)
    wanted = [[b * heads + h for h in range(heads)] for b in range(nb)]
    for name, ref in (("growth", growth_ref), ("beyond", beyond_ref)):
        for b, a in enumerate(spread(fac.all(name), wanted, heads * e)):
            ref[b * BLK : (b + 1) * BLK, :] = a
    fetch[0].wait()
    for b in range(nb):
        causal, decays = fac.decays(b)
        for h in range(heads):
            q = block(q_ref, b, h, e)
            scores = mm(q, block(k_ref, b, h, e), NT)
            weights = jnp.where(causal, scores * decays[h], 0.0).astype(BF16)
            w_ref[b, h] = weights
            within_ref[b * BLK : (b + 1) * BLK, h * e : (h + 1) * e] = mm(
                weights, block(v_ref, b, h, e)
            )
            lifted_ref[b, h] = (q.T.astype(F32) * fac.row("growth", b, h)).astype(BF16)
    fetch[1].wait()


def row_sums(a):
    width = a.shape[1]
    narrow = sum(a[:, i : i + LANES] for i in range(0, width, LANES))
    return jnp.sum(narrow.T, axis=0, keepdims=True)


def attend_kernel(
    dims, masks, factors_ref, q_ref, cot_ref, within_ref, growth_ref, local_ref, *refs
):
    payloads, (held_ref, att_ref, sums_ref) = refs[: len(masks)], refs[len(masks) :]
    nb, heads, e = dims
    fac = Factors(factors_ref, nb, heads)
    for h in range(heads):
        arrived = incoming(payloads, lax.axis_index("ctx"), masks, h, e, heads, False)
        ahead = jnp.zeros((1, e), F32)
        for b in range(nb):
            state = jnp.exp(ahead) * arrived
            if b:
                state = state + local_ref[b - 1, h]
            ahead = ahead + fac.row("total", b, h, e)
            held_ref[b, h] = state.astype(BF16)
    squares, crosses = [], []
    for b in range(nb):
        rows = slice(b * BLK, (b + 1) * BLK)
        carried = jnp.concatenate(
            [mm(block(q_ref, b, h, e), held_ref[b, h]) for h in range(heads)], axis=1
        )
        att = within_ref[rows, :] + growth_ref[rows, :] * carried
        att_ref[rows, :] = att
        squares.append(row_sums(att * att))
        crosses.append(row_sums(att * cot_ref[rows, :].astype(F32)))
    parts = squares + crosses
    if up8(2 * nb) > 2 * nb:
        parts.append(jnp.zeros((up8(2 * nb) - 2 * nb, BLK), F32))
    sums_ref[...] = jnp.concatenate(parts, axis=0)


def grad_kernel(dims, full_width, parts, factors_ref, lifted_ref, cot_ref, att_ref, *refs):
    sums_refs, (g_ref, scale_ref, payload_ref, local_ref) = refs[:parts], refs[parts:]
    nb, heads, e = dims
    fac = Factors(factors_ref, nb, heads)
    sums = sum(ref[...] for ref in sums_refs)
    squares = jnp.where(iota(sums.shape, 0) < nb, sums, 0.0)
    scale = lax.rsqrt(squares / full_width + EPSILON)
    scale_ref[...] = scale
    squared = scale * scale
    lean = jnp.concatenate([squared[:nb], squared[:nb], squared[2 * nb :]], axis=0) * sums / full_width
    factors = jnp.where(iota(sums.shape, 0) < nb, scale, lean)
    columns = spread(factors, [[r] for r in range(2 * nb)], e)
    running = [None] * heads
    for b in reversed(range(nb)):
        rows = slice(b * BLK, (b + 1) * BLK)
        for h in range(heads):
            cols = slice(h * e, (h + 1) * e)
            g = columns[b] * (cot_ref[rows, cols].astype(F32) - att_ref[rows, cols] * columns[nb + b])
            g = g.astype(BF16)
            g_ref[rows, cols] = g
            term = mm(lifted_ref[b, h], g)
            running[h] = term if b == nb - 1 else fac.row("decay", b, h, e) * running[h] + term
            if b:
                local_ref[b - 1, h] = running[h]
    for h in range(heads):
        payload_ref[h * e : (h + 1) * e, :] = running[h]
    store_totals(payload_ref, fac, e)


def inner_grads_kernel(
    dims, factors_ref, q_ref, k_ref, v_ref, g_ref, w_ref, held_ref, att_ref, growth_ref, scale_ref,
    out_hbm, gq_hbm, gk_ref, gv_ref, out_ref, gq_ref, sems,
):
    nb, heads, e = dims
    fac = Factors(factors_ref, nb, heads)
    scale = spread(scale_ref[...], [[b] for b in range(nb)], heads * e)
    copies = []
    for b in range(nb):
        rows = slice(b * BLK, (b + 1) * BLK)
        out_ref[rows, :] = (att_ref[rows, :] * scale[b]).astype(BF16)
        copies.append(
            pltpu.make_async_copy(out_ref.at[rows], out_hbm.at[rows], sems.at[2 * b])
        )
        copies[-1].start()
        causal, decays = fac.decays(b)
        for h in range(heads):
            cols = slice(h * e, (h + 1) * e)
            g = block(g_ref, b, h, e)
            scores = mm(g, block(v_ref, b, h, e), NT)
            gw = jnp.where(causal, scores * decays[h], 0.0).astype(BF16)
            gq = mm(gw, block(k_ref, b, h, e)) + growth_ref[rows, cols] * mm(g, held_ref[b, h], NT)
            gq_ref[rows, cols] = gq.astype(BF16)
            gk_ref[rows, cols] = mm(gw, block(q_ref, b, h, e), TN)
            gv_ref[rows, cols] = mm(w_ref[b, h], g, TN)
        copies.append(
            pltpu.make_async_copy(gq_ref.at[rows], gq_hbm.at[rows], sems.at[2 * b + 1])
        )
        copies[-1].start()
    for c in copies:
        c.wait()


def outer_grads_kernel(
    dims, masks, factors_ref, k_ref, v_ref, gk_part_ref, gv_part_ref, beyond_ref, local_ref, *refs
):
    payloads, (gk_hbm, gv_hbm, gk_ref, gv_ref, sems) = refs[: len(masks)], refs[len(masks) :]
    nb, heads, e = dims
    fac = Factors(factors_ref, nb, heads)
    arrived = [incoming(payloads, lax.axis_index("ctx"), masks, h, e, heads, True) for h in range(heads)]
    behind = [jnp.zeros((1, e), F32) for h in range(heads)]
    copies = []
    for b in reversed(range(nb)):
        rows = slice(b * BLK, (b + 1) * BLK)
        held = []
        for h in range(heads):
            state = jnp.exp(behind[h]) * arrived[h]
            if b < nb - 1:
                state = state + local_ref[b, h]
            behind[h] = behind[h] + fac.row("total", b, h, e)
            held.append(state.astype(BF16))
        for i, (of, part, s, d) in enumerate(
            ((v_ref, gk_part_ref, gk_ref, gk_hbm), (k_ref, gv_part_ref, gv_ref, gv_hbm))
        ):
            for h in range(heads):
                cols = slice(h * e, (h + 1) * e)
                far = mm(block(of, b, h, e), held[h], NN if i else NT)
                s[rows, cols] = (part[rows, cols] + beyond_ref[rows, cols] * far).astype(BF16)
            copies.append(pltpu.make_async_copy(s.at[rows], d.at[rows], sems.at[2 * b + i]))
            copies[-1].start()
    for c in copies:
        c.wait()


def call(kernel, name, args, outs, flops, hbm_ins=0, hbm_outs=0, scratch=()):
    traffic = sum(a.size * a.dtype.itemsize for a in args) + sum(
        math.prod(s) * jnp.dtype(d).itemsize for s, d in outs
    )
    hbm = pl.BlockSpec(memory_space=pltpu.HBM)
    vmem = pl.BlockSpec(memory_space=pltpu.VMEM)
    args = [
        pltpu.with_memory_space_constraint(a, pltpu.HBM) if i < hbm_ins else a for i, a in enumerate(args)
    ]
    return pl.pallas_call(
        kernel,
        out_shape=[(pltpu.HBM if i < hbm_outs else pltpu.VMEM)(s, d) for i, (s, d) in enumerate(outs)],
        in_specs=[hbm if i < hbm_ins else vmem for i in range(len(args))],
        out_specs=[hbm if i < hbm_outs else vmem for i in range(len(outs))],
        scratch_shapes=scratch,
        compiler_params=pltpu.CompilerParams(vmem_limit_bytes=16 * 2**20),
        cost_estimate=pl.CostEstimate(flops=flops, bytes_accessed=traffic, transcendentals=0),
        name=name,
    )(*args)


def nothing(*refs):
    pass


def after(a, other):
    anywhere = pl.BlockSpec(memory_space=pltpu.VMEM)
    return pl.pallas_call(
        nothing,
        out_shape=pltpu.VMEM(a.shape, a.dtype),
        in_specs=[anywhere, anywhere],
        out_specs=anywhere,
        input_output_aliases={0: 0},
        compiler_params=pltpu.CompilerParams(vmem_limit_bytes=4 * 2**20),
        name="after",
    )(a, other)


def swap(a, axis, mask):
    return lax.ppermute(a, axis, [(i, i ^ mask) for i in range(lax.axis_size(axis))])


def gather_states(payload, work):
    bit = lax.axis_size("ctx") // 2
    first = swap(payload, "ctx", bit) if bit else payload
    done = work()
    first = after(first, done[-1])
    masks, held = ([0, bit], [payload, first]) if bit else ([0], [payload])
    bit //= 2
    while bit:
        held += [swap(a, "ctx", bit) for a in held]
        masks += [m | bit for m in masks]
        bit //= 2
    return masks, held, done


def sum_over_heads(sums):
    size = lax.axis_size("head")
    rounds = [range(1, min(4, size))] + [[bit] for bit in (4, 8, 16, 32, 64, 128) if bit < size]
    parts = [sums]
    for apart in rounds:
        own = functools.reduce(jnp.add, parts)
        parts = [own] + [swap(own, "head", k) for k in apart]
    return parts


def shards(queries, keys, values, cotangent, decay_code, boundaries):
    tokens, width = queries.shape
    heads = decay_code.shape[0]
    e = width // heads
    nb = tokens // BLK
    dims = (nb, heads, e)
    full_width = width * lax.axis_size("head")
    bnd = boundaries.reshape(tokens // LANES, LANES)
    payload = ((heads * e + up8(heads), LANES), F32)
    local = ((max(nb - 1, 1), heads, e, e), F32)
    narrow, wide = ((tokens, width), BF16), ((tokens, width), F32)
    stage = [pltpu.VMEM((tokens, width), BF16)] * 2 + [pltpu.SemaphoreType.DMA((2 * nb,))]
    big = 2 * tokens * heads * e * BLK
    small = 2 * tokens * heads * e * e

    state, prefix, factors, k, v = call(
        functools.partial(states_kernel, dims), "states", (decay_code, bnd, keys, values),
        (payload, local, ((len(ROWS) * up8(nb * heads), BLK), F32), narrow, narrow), small, hbm_ins=4,
        scratch=(pltpu.SMEM((heads,), jnp.int32), pltpu.VMEM(bnd.shape, jnp.int32), pltpu.SemaphoreType.DMA((4,))),
    )
    masks, states, (weights, within, growth, beyond, lifted, q, cot) = gather_states(state, lambda: call(
        functools.partial(within_kernel, dims), "within", (queries, cotangent, factors, k, v),
        (((nb, heads, BLK, BLK), BF16), wide, wide, wide, ((nb, heads, e, BLK), BF16), narrow, narrow), 2 * big,
        hbm_ins=2, scratch=(pltpu.SemaphoreType.DMA((2,)),),
    ))
    held, attended, sums = call(
        functools.partial(attend_kernel, dims, masks), "attend",
        (factors, q, cot, within, growth, prefix, *states),
        (((nb, heads, e, e), BF16), wide, ((up8(2 * nb), BLK), F32)), small,
    )
    sums = sum_over_heads(sums)
    grad, scale, grad_state, suffix = call(
        functools.partial(grad_kernel, dims, full_width, len(sums)), "grad",
        (factors, lifted, cot, attended, *sums),
        (narrow, ((up8(2 * nb), BLK), F32), payload, local), small,
    )
    masks, grad_states, (output, grad_queries, gk_part, gv_part) = gather_states(grad_state, lambda: call(
        functools.partial(inner_grads_kernel, dims), "inner_grads",
        (factors, q, k, v, grad, weights, held, attended, growth, scale),
        (narrow, narrow, wide, wide), 4 * big + small, hbm_outs=2, scratch=stage,
    ))
    grad_keys, grad_values = call(
        functools.partial(outer_grads_kernel, dims, masks), "outer_grads",
        (factors, k, v, gk_part, gv_part, beyond, suffix, *grad_states),
        (narrow, narrow), 2 * small, hbm_outs=2, scratch=stage,
    )
    return output, grad_queries, grad_keys, grad_values


def solution(mesh):
    both = P("ctx", "head")
    return jax.shard_map(
        shards,
        mesh=mesh,
        in_specs=(both, both, both, both, P("head"), P("ctx")),
        out_specs=(both, both, both, both),
        check_vma=False,
    )
```

```python
import functools
import math

import jax
import jax.numpy as jnp
from jax import lax
from jax.experimental import pallas as pl
from jax.experimental.pallas import tpu as pltpu
from jax.sharding import PartitionSpec as P

BLK = 256
LANES = 128
LOG_TWO = math.log(2.0)
EPSILON = 1e-06
F32 = jnp.float32
BF16 = jnp.bfloat16

NN = (((1,), (0,)), ((), ()))
NT = (((1,), (1,)), ((), ()))
TN = (((0,), (0,)), ((), ()))


def mm(a, b, dims=NN):
    return lax.dot_general(a, b, dims, preferred_element_type=F32)


def iota(shape, axis):
    return lax.broadcasted_iota(jnp.int32, shape, axis)


def up8(n):
    return -(-n // 8) * 8


def halves(x):
    head = x.astype(BF16)
    return head, (x - head.astype(F32)).astype(BF16)


ROWS = ("growth", "beyond", "decay", "total", "count", "rate")


def factor_rows(bnd_ref, code_ref, blocks, heads):
    rows = up8(blocks * heads)
    per = BLK // LANES
    bnd = bnd_ref[...].astype(F32)
    parts = []
    for b in range(blocks):
        row = jnp.concatenate([bnd[b * per + i : b * per + i + 1] for i in range(per)], axis=1)
        parts += [row] * heads
    if rows > blocks * heads:
        parts.append(jnp.zeros((rows - blocks * heads, BLK), F32))
    marks = jnp.concatenate(parts, axis=0).astype(BF16)
    upper = (iota((BLK, BLK), 0) <= iota((BLK, BLK), 1)).astype(F32).astype(BF16)
    count = mm(marks, upper)
    count_all = mm(marks, jnp.ones((BLK, BLK), BF16))
    which = iota((rows, BLK), 0)
    code = jnp.zeros((rows, BLK), F32)
    for h in range(heads):
        code = jnp.where(which % heads == h, code_ref[h].astype(F32), code)
    rate = jnp.log1p(code * -(2.0 ** (-20)))
    place = (iota((rows, BLK), 1) + 1).astype(F32)
    level = rate * place - LOG_TWO * count
    total = rate * float(BLK) - LOG_TWO * count_all
    return jnp.exp(level), jnp.exp(total - level), jnp.exp(total), total, count, rate


class Factors:
    def __init__(self, ref, blocks, heads):
        self.ref, self.blocks, self.heads, self.rows = ref, blocks, heads, up8(blocks * heads)

    def all(self, name):
        at = ROWS.index(name) * self.rows
        return self.ref[at : at + self.rows, :]

    def row(self, name, b, h, lanes=BLK):
        at = ROWS.index(name) * self.rows + b * self.heads + h
        return self.ref[at : at + 1, :lanes]

    def device_total(self, h):
        return sum(self.row("total", b, h, LANES) for b in range(self.blocks))

    def decays(self, b):
        pick = (iota((self.rows, BLK), 0) == b * self.heads).astype(F32).astype(BF16)
        count_i = mm(self.all("count").astype(BF16), pick, TN)
        halved = LOG_TWO * (count_i - self.row("count", b, 0))
        apart = iota((BLK, BLK), 0) - iota((BLK, BLK), 1)
        causal = apart >= 0
        steps = apart.astype(F32)
        return causal, [
            jnp.exp(jnp.where(causal, self.row("rate", b, h) * steps - halved, 0.0))
            for h in range(self.heads)
        ]


def spread(a, wanted, width):
    head, rest = halves(a)
    both = jnp.concatenate([head.astype(F32), rest.astype(F32)], axis=0).T.astype(BF16)
    rows = a.shape[0]
    result = []
    for some in wanted:
        lane, row = iota((2 * rows, width), 1), iota((2 * rows, width), 0) % rows
        pick = jnp.zeros((2 * rows, width), F32)
        for i, r in enumerate(some):
            share = lane // (width // len(some)) == i
            pick = jnp.where(jnp.logical_and(share, row == r), 1.0, pick)
        result.append(mm(both, pick.astype(BF16)))
    return result


def incoming(payloads, place, masks, h, head_size, heads, reverse):
    at = heads * head_size + h
    totals = [p[at : at + 1, :] for p in payloads]
    sources = [place ^ m for m in masks]

    def before(a, b):
        return a > b if reverse else a < b

    result = jnp.zeros((head_size, head_size), F32)
    for i, m in enumerate(masks):
        if m == 0:
            continue
        inner = jnp.zeros_like(totals[0])
        for j, other in enumerate(masks):
            if other in (0, m):
                continue
            between = jnp.logical_and(before(sources[i], sources[j]), before(sources[j], place))
            inner = inner + jnp.where(between, totals[j], 0.0)
        weight = jnp.where(before(sources[i], place), jnp.exp(inner), 0.0)
        result = result + weight * payloads[i][h * head_size : (h + 1) * head_size, :]
    return result


def store_totals(payload_ref, fac, head_size):
    rest = [fac.device_total(h) for h in range(fac.heads)]
    pad = up8(fac.heads) - fac.heads
    if pad:
        rest.append(jnp.zeros((pad, LANES), F32))
    payload_ref[fac.heads * head_size :, :] = jnp.concatenate(rest, axis=0)


def block(ref, b, h, e):
    return ref[b * BLK : (b + 1) * BLK, h * e : (h + 1) * e]


def states_kernel(
    dims, code_in, bnd_in, k_in, v_in,
    payload_ref, local_ref, factors_ref, k_ref, v_ref, code_ref, bnd_ref, sems,
):
    nb, heads, e = dims
    fetch = [
        pltpu.make_async_copy(s, d, sems.at[i])
        for i, (s, d) in enumerate(((code_in, code_ref), (bnd_in, bnd_ref)))
    ]
    for s, d in ((k_in, k_ref), (v_in, v_ref)):
        fetch.append(pltpu.make_async_copy(s, d, sems.at[len(fetch)]))
    for c in fetch:
        c.start()
    fetch[0].wait()
    fetch[1].wait()
    made = factor_rows(bnd_ref, code_ref, nb, heads)
    rows = up8(nb * heads)
    for i, a in enumerate(made):
        factors_ref[i * rows : (i + 1) * rows, :] = a
    fac = Factors(factors_ref, nb, heads)
    store_totals(payload_ref, fac, e)
    fetch[2].wait()
    fetch[3].wait()
    for h in range(heads):
        running = None
        for b in range(nb):
            scaled = (block(k_ref, b, h, e).T.astype(F32) * fac.row("beyond", b, h)).astype(BF16)
            term = mm(scaled, block(v_ref, b, h, e))
            running = term if running is None else fac.row("decay", b, h, e) * running + term
            if b < nb - 1:
                local_ref[b, h] = running
        payload_ref[h * e : (h + 1) * e, :] = running


def within_kernel(
    dims, q_in, cot_in, factors_ref, k_ref, v_ref,
    w_ref, within_ref, growth_ref, beyond_ref, lifted_ref, q_ref, cot_ref, sems,
):
    nb, heads, e = dims
    fetch = [
        pltpu.make_async_copy(s, d, sems.at[i])
        for i, (s, d) in enumerate(((q_in, q_ref), (cot_in, cot_ref)))
    ]
    for c in fetch:
        c.start()
    fac = Factors(factors_ref, nb, heads)
    wanted = [[b * heads + h for h in range(heads)] for b in range(nb)]
    for name, ref in (("growth", growth_ref), ("beyond", beyond_ref)):
        for b, a in enumerate(spread(fac.all(name), wanted, heads * e)):
            ref[b * BLK : (b + 1) * BLK, :] = a
    fetch[0].wait()
    for b in range(nb):
        causal, decays = fac.decays(b)
        for h in range(heads):
            q = block(q_ref, b, h, e)
            scores = mm(q, block(k_ref, b, h, e), NT)
            weights = jnp.where(causal, scores * decays[h], 0.0).astype(BF16)
            w_ref[b, h] = weights
            within_ref[b * BLK : (b + 1) * BLK, h * e : (h + 1) * e] = mm(
                weights, block(v_ref, b, h, e)
            )
            lifted_ref[b, h] = (q.T.astype(F32) * fac.row("growth", b, h)).astype(BF16)
    fetch[1].wait()


def row_sums(a):
    width = a.shape[1]
    narrow = sum(a[:, i : i + LANES] for i in range(0, width, LANES))
    return jnp.sum(narrow.T, axis=0, keepdims=True)


def attend_kernel(
    dims, masks, factors_ref, q_ref, cot_ref, within_ref, growth_ref, local_ref, *refs
):
    payloads, (held_ref, att_ref, sums_ref) = refs[: len(masks)], refs[len(masks) :]
    nb, heads, e = dims
    fac = Factors(factors_ref, nb, heads)
    for h in range(heads):
        arrived = incoming(payloads, lax.axis_index("ctx"), masks, h, e, heads, False)
        ahead = jnp.zeros((1, e), F32)
        for b in range(nb):
            state = jnp.exp(ahead) * arrived
            if b:
                state = state + local_ref[b - 1, h]
            ahead = ahead + fac.row("total", b, h, e)
            held_ref[b, h] = state.astype(BF16)
    squares, crosses = [], []
    for b in range(nb):
        rows = slice(b * BLK, (b + 1) * BLK)
        square = cross = 0.0
        for h in range(heads):
            cols = slice(h * e, (h + 1) * e)
            carried = mm(block(q_ref, b, h, e), held_ref[b, h])
            att = within_ref[rows, cols] + growth_ref[rows, cols] * carried
            att_ref[rows, cols] = att
            square = square + att * att
            cross = cross + att * cot_ref[rows, cols].astype(F32)
        squares.append(row_sums(square))
        crosses.append(row_sums(cross))
    parts = squares + crosses
    if up8(2 * nb) > 2 * nb:
        parts.append(jnp.zeros((up8(2 * nb) - 2 * nb, BLK), F32))
    sums_ref[...] = jnp.concatenate(parts, axis=0)


def grad_kernel(dims, full_width, parts, factors_ref, lifted_ref, cot_ref, att_ref, *refs):
    sums_refs, (g_ref, scale_ref, payload_ref, local_ref) = refs[:parts], refs[parts:]
    nb, heads, e = dims
    fac = Factors(factors_ref, nb, heads)
    sums = sum(ref[...] for ref in sums_refs)
    squares = jnp.where(iota(sums.shape, 0) < nb, sums, 0.0)
    scale = lax.rsqrt(squares / full_width + EPSILON)
    scale_ref[...] = scale
    squared = scale * scale
    lean = jnp.concatenate([squared[:nb], squared[:nb], squared[2 * nb :]], axis=0) * sums / full_width
    factors = jnp.where(iota(sums.shape, 0) < nb, scale, lean)
    columns = spread(factors, [[r] for r in range(2 * nb)], e)
    running = [None] * heads
    for b in reversed(range(nb)):
        rows = slice(b * BLK, (b + 1) * BLK)
        for h in range(heads):
            cols = slice(h * e, (h + 1) * e)
            g = columns[b] * (cot_ref[rows, cols].astype(F32) - att_ref[rows, cols] * columns[nb + b])
            g = g.astype(BF16)
            g_ref[rows, cols] = g
            term = mm(lifted_ref[b, h], g)
            running[h] = term if b == nb - 1 else fac.row("decay", b, h, e) * running[h] + term
            if b:
                local_ref[b - 1, h] = running[h]
    for h in range(heads):
        payload_ref[h * e : (h + 1) * e, :] = running[h]
    store_totals(payload_ref, fac, e)


def inner_grads_kernel(
    dims, factors_ref, q_ref, k_ref, v_ref, g_ref, w_ref, held_ref, att_ref, growth_ref, scale_ref,
    out_hbm, gq_hbm, gk_ref, gv_ref, out_ref, gq_ref, sems,
):
    nb, heads, e = dims
    fac = Factors(factors_ref, nb, heads)
    scale = spread(scale_ref[...], [[b] for b in range(nb)], heads * e)
    copies = []
    for b in range(nb):
        rows = slice(b * BLK, (b + 1) * BLK)
        out_ref[rows, :] = (att_ref[rows, :] * scale[b]).astype(BF16)
        copies.append(
            pltpu.make_async_copy(out_ref.at[rows], out_hbm.at[rows], sems.at[2 * b])
        )
        copies[-1].start()
        causal, decays = fac.decays(b)
        for h in range(heads):
            cols = slice(h * e, (h + 1) * e)
            g = block(g_ref, b, h, e)
            scores = mm(g, block(v_ref, b, h, e), NT)
            gw = jnp.where(causal, scores * decays[h], 0.0).astype(BF16)
            gq = mm(gw, block(k_ref, b, h, e)) + growth_ref[rows, cols] * mm(g, held_ref[b, h], NT)
            gq_ref[rows, cols] = gq.astype(BF16)
            gk_ref[rows, cols] = mm(gw, block(q_ref, b, h, e), TN)
            gv_ref[rows, cols] = mm(w_ref[b, h], g, TN)
        copies.append(
            pltpu.make_async_copy(gq_ref.at[rows], gq_hbm.at[rows], sems.at[2 * b + 1])
        )
        copies[-1].start()
    for c in copies:
        c.wait()


def outer_grads_kernel(
    dims, masks, factors_ref, k_ref, v_ref, gk_part_ref, gv_part_ref, beyond_ref, local_ref, *refs
):
    payloads, (gk_hbm, gv_hbm, gk_ref, gv_ref, sems) = refs[: len(masks)], refs[len(masks) :]
    nb, heads, e = dims
    fac = Factors(factors_ref, nb, heads)
    arrived = [incoming(payloads, lax.axis_index("ctx"), masks, h, e, heads, True) for h in range(heads)]
    behind = [jnp.zeros((1, e), F32) for h in range(heads)]
    copies = []
    for b in reversed(range(nb)):
        rows = slice(b * BLK, (b + 1) * BLK)
        held = []
        for h in range(heads):
            state = jnp.exp(behind[h]) * arrived[h]
            if b < nb - 1:
                state = state + local_ref[b, h]
            behind[h] = behind[h] + fac.row("total", b, h, e)
            held.append(state.astype(BF16))
        for i, (of, part, s, d) in enumerate(
            ((v_ref, gk_part_ref, gk_ref, gk_hbm), (k_ref, gv_part_ref, gv_ref, gv_hbm))
        ):
            for h in range(heads):
                cols = slice(h * e, (h + 1) * e)
                far = mm(block(of, b, h, e), held[h], NN if i else NT)
                s[rows, cols] = (part[rows, cols] + beyond_ref[rows, cols] * far).astype(BF16)
            copies.append(pltpu.make_async_copy(s.at[rows], d.at[rows], sems.at[2 * b + i]))
            copies[-1].start()
    for c in copies:
        c.wait()


def call(kernel, name, args, outs, flops, hbm_ins=0, hbm_outs=0, scratch=()):
    traffic = sum(a.size * a.dtype.itemsize for a in args) + sum(
        math.prod(s) * jnp.dtype(d).itemsize for s, d in outs
    )
    hbm = pl.BlockSpec(memory_space=pltpu.HBM)
    vmem = pl.BlockSpec(memory_space=pltpu.VMEM)
    args = [
        pltpu.with_memory_space_constraint(a, pltpu.HBM) if i < hbm_ins else a for i, a in enumerate(args)
    ]
    return pl.pallas_call(
        kernel,
        out_shape=[(pltpu.HBM if i < hbm_outs else pltpu.VMEM)(s, d) for i, (s, d) in enumerate(outs)],
        in_specs=[hbm if i < hbm_ins else vmem for i in range(len(args))],
        out_specs=[hbm if i < hbm_outs else vmem for i in range(len(outs))],
        scratch_shapes=scratch,
        compiler_params=pltpu.CompilerParams(vmem_limit_bytes=16 * 2**20),
        cost_estimate=pl.CostEstimate(flops=flops, bytes_accessed=traffic, transcendentals=0),
        name=name,
    )(*args)


def nothing(*refs):
    pass


def after(a, other):
    anywhere = pl.BlockSpec(memory_space=pltpu.VMEM)
    return pl.pallas_call(
        nothing,
        out_shape=pltpu.VMEM(a.shape, a.dtype),
        in_specs=[anywhere, anywhere],
        out_specs=anywhere,
        input_output_aliases={0: 0},
        compiler_params=pltpu.CompilerParams(vmem_limit_bytes=4 * 2**20),
        name="after",
    )(a, other)


def swap(a, axis, mask):
    return lax.ppermute(a, axis, [(i, i ^ mask) for i in range(lax.axis_size(axis))])


def gather_states(payload, work):
    bit = lax.axis_size("ctx") // 2
    first = swap(payload, "ctx", bit) if bit else payload
    done = work()
    first = after(first, done[-1])
    masks, held = ([0, bit], [payload, first]) if bit else ([0], [payload])
    bit //= 2
    while bit:
        held += [swap(a, "ctx", bit) for a in held]
        masks += [m | bit for m in masks]
        bit //= 2
    return masks, held, done


def sum_over_heads(sums):
    size = lax.axis_size("head")
    rounds = [range(1, min(4, size))] + [[bit] for bit in (4, 8, 16, 32, 64, 128) if bit < size]
    parts = [sums]
    for apart in rounds:
        own = functools.reduce(jnp.add, parts)
        parts = [own] + [swap(own, "head", k) for k in apart]
    return parts


def shards(queries, keys, values, cotangent, decay_code, boundaries):
    tokens, width = queries.shape
    heads = decay_code.shape[0]
    e = width // heads
    nb = tokens // BLK
    dims = (nb, heads, e)
    full_width = width * lax.axis_size("head")
    bnd = boundaries.reshape(tokens // LANES, LANES)
    payload = ((heads * e + up8(heads), LANES), F32)
    local = ((max(nb - 1, 1), heads, e, e), F32)
    narrow, wide = ((tokens, width), BF16), ((tokens, width), F32)
    stage = [pltpu.VMEM((tokens, width), BF16)] * 2 + [pltpu.SemaphoreType.DMA((2 * nb,))]
    big = 2 * tokens * heads * e * BLK
    small = 2 * tokens * heads * e * e

    state, prefix, factors, k, v = call(
        functools.partial(states_kernel, dims), "states", (decay_code, bnd, keys, values),
        (payload, local, ((len(ROWS) * up8(nb * heads), BLK), F32), narrow, narrow), small, hbm_ins=4,
        scratch=(pltpu.SMEM((heads,), jnp.int32), pltpu.VMEM(bnd.shape, jnp.int32), pltpu.SemaphoreType.DMA((4,))),
    )
    masks, states, (weights, within, growth, beyond, lifted, q, cot) = gather_states(state, lambda: call(
        functools.partial(within_kernel, dims), "within", (queries, cotangent, factors, k, v),
        (((nb, heads, BLK, BLK), BF16), wide, wide, wide, ((nb, heads, e, BLK), BF16), narrow, narrow), 2 * big,
        hbm_ins=2, scratch=(pltpu.SemaphoreType.DMA((2,)),),
    ))
    held, attended, sums = call(
        functools.partial(attend_kernel, dims, masks), "attend",
        (factors, q, cot, within, growth, prefix, *states),
        (((nb, heads, e, e), BF16), wide, ((up8(2 * nb), BLK), F32)), small,
    )
    sums = sum_over_heads(sums)
    grad, scale, grad_state, suffix = call(
        functools.partial(grad_kernel, dims, full_width, len(sums)), "grad",
        (factors, lifted, cot, attended, *sums),
        (narrow, ((up8(2 * nb), BLK), F32), payload, local), small,
    )
    masks, grad_states, (output, grad_queries, gk_part, gv_part) = gather_states(grad_state, lambda: call(
        functools.partial(inner_grads_kernel, dims), "inner_grads",
        (factors, q, k, v, grad, weights, held, attended, growth, scale),
        (narrow, narrow, wide, wide), 4 * big + small, hbm_outs=2, scratch=stage,
    ))
    grad_keys, grad_values = call(
        functools.partial(outer_grads_kernel, dims, masks), "outer_grads",
        (factors, k, v, gk_part, gv_part, beyond, suffix, *grad_states),
        (narrow, narrow), 2 * small, hbm_outs=2, scratch=stage,
    )
    return output, grad_queries, grad_keys, grad_values


def solution(mesh):
    both = P("ctx", "head")
    return jax.shard_map(
        shards,
        mesh=mesh,
        in_specs=(both, both, both, both, P("head"), P("ctx")),
        out_specs=(both, both, both, both),
        check_vma=False,
    )
```
